32 devices in a mesh: gx: 4 (over z), gy: 4 (over y, x), gz: 2 (over core).
Axes of the slice: x: 2, y: 2, z: 4, core: 2. Of those that a mesh axis runs over, the one named last changes fastest.
Arguments:
- field: float32 [4, 256, 128, 1024], P(None, 'gx', 'gz', 'gy'), may hold values from -6 to 6
- basis_two: float32 [1024, 64], P('gy'), may hold values from -0.1875 to 0.1875
- basis_three: float32 [128, 64], P('gz'), may hold values from -0.5 to 0.5
Outputs:
- projected: float32 [256, 16384], P('gx', ('gy', 'gz'))
- gram: float32 [256, 256], P('gx')
The draws below stay inside these ranges and needn't reach their ends.
All inputs are finite; a program needn't handle non-finite values.
Results may differ from the reference program's by a relative error of at most 0.000071.
Values sent between devices are 32-bit elements; how exact they have to be, the bound alone decides.
A program may use at most 128 MiB of HBM per device.

```python
import jax
import jax.numpy as jnp
from jax import lax

V = 4
R = 64
N1 = 256
N2 = 1024
N3 = 128
K = 16384


def block_levels(stream_key, dims, split, smallest, top_value):
    level, own = 1.0, jax.random.fold_in(stream_key, 6)
    for axis_at, shards_of in split:
        heights = jnp.exp(jax.random.uniform(jax.random.fold_in(own, axis_at), (shards_of,), jnp.float32, smallest / len(split), top_value / len(split)))
        level = level * jnp.repeat(heights, dims[axis_at] // shards_of).reshape([-1 if axis == axis_at else 1 for axis in range(len(dims))])
    return level


def scatter_about(stream_key, shape, width, limit, cuts=(), held_as=jnp.bfloat16):
    values = jax.random.normal(stream_key, shape, jnp.float32) * width
    if len(cuts) > 0:
        values = block_levels(stream_key, shape, cuts, -0.22, 0.18) * values
    return jnp.clip(values, min=-limit, max=limit).astype(held_as)


def setup_inputs(seed: int = 0) -> dict:
    splits = jax.random.split(jax.random.key(seed), 4)
    field = scatter_about(splits[0], (V, N1, N3, N2), 1.0, 6.0, ((1, 4), (2, 2), (3, 4)), jnp.float32)
    basis_two = scatter_about(splits[1], (N2, R), N2 ** -0.5, 0.1875, ((0, 4),), jnp.float32)
    basis_three = scatter_about(splits[2], (N3, R), N3 ** -0.5, 0.5, ((0, 2),), jnp.float32)
    return dict(field=field, basis_two=basis_two, basis_three=basis_three)


def reference(field, basis_two, basis_three):
    hp = lax.Precision.HIGHEST
    first = jnp.einsum("vacb,bs->vacs", field, basis_two, precision=hp)
    core = jnp.einsum("vacs,ct->avst", first, basis_three, precision=hp)
    projected = core.reshape(core.shape[0], -1)
    gram = jnp.dot(projected, projected.T, precision=hp, preferred_element_type=jnp.float32) / jnp.float32(K)
    return projected, gram
```

```python
import functools

import jax
import jax.numpy as jnp
from jax import lax
from jax.experimental import pallas as pl
from jax.experimental.pallas import tpu as pltpu
from jax.sharding import PartitionSpec as P

MESH = pl.DeviceIdType.MESH
F32 = jnp.float32
BF16 = jnp.bfloat16
CHUNKS = 4
LANES = 128


def split(x):
    high = x.astype(BF16)
    return high, (x - high.astype(F32)).astype(BF16)


def mul(a, b):
    return lax.dot_general(a, b, (((1,), (0,)), ((), ())), preferred_element_type=F32)


def mul_t(a, b):
    return lax.dot_general(a, b, (((1,), (1,)), ((), ())), preferred_element_type=F32)


def kernel(shape, gsize, field, b2_ref, b3_ref, proj, gram, *scratch):
    (fbuf, w2, k3, k3f, core, rgz, half, rgy, xbuf, q1, q2, tbuf, t1, t2, gp, rg, fin,
     fsem, zs, zr, ys, yr, as_, ar, bs, br, ts, tr, gs, gr, hs, hr) = scratch
    nv, rows, depth, width = shape
    GX, GY, GZ = gsize
    rank = b2_ref.shape[1]
    tdim = b3_ref.shape[1]
    step = rows // CHUNKS
    pairs = step // 2
    sloc = rank // GZ
    cols = sloc * tdim
    nr = GY * GZ
    slab = rows // nr
    gx, gy, gz = lax.axis_index("gx"), lax.axis_index("gy"), lax.axis_index("gz")
    me = gy * GZ + gz

    def layer(d):
        other = lax.rem(me + d, nr)
        return other, (gx, other // GZ, lax.rem(other, GZ))

    loads = [
        pltpu.make_async_copy(
            field.at[:, pl.ds(k * step, step)], fbuf.at[:, pl.ds(k * step, step)], fsem.at[k]
        )
        for k in range(CHUNKS)
    ]
    for load in loads:
        load.start()

    barrier = pltpu.get_barrier_semaphore()
    for d in range(1, nr):
        pl.semaphore_signal(barrier, inc=1, device_id=layer(d)[1], device_id_type=MESH)
    for d in range(1, GX):
        pl.semaphore_signal(
            barrier, inc=1, device_id=(lax.rem(gx + d, GX), gy, gz), device_id_type=MESH
        )

    high, low = split(b2_ref[...].T)
    w2[0:rank, :] = high
    w2[rank : 2 * rank, :] = low
    k3f[...] = jnp.zeros_like(k3f)
    for i in range(4):
        k3f[i * depth : (i + 1) * depth, i * tdim : (i + 1) * tdim] = b3_ref[...]
    high, low = split(k3f[...])
    k3[0] = high
    k3[1] = low

    def contract(k):
        @pl.loop(0, pairs // 2)
        def _(j):
            base = k * step + 2 * j
            parts = []
            for v in range(nv):
                tile = jnp.concatenate(
                    [fbuf[v, base + o] for o in (0, pairs, 1, pairs + 1)], axis=0
                )
                high, low = split(tile)
                one = mul_t(w2[...], high)
                two = mul_t(w2[0:rank, :], low)
                parts.append(one[0:rank] + one[rank:] + two)
            high, low = split(jnp.concatenate(parts, axis=0))
            c = mul(high, k3[0]) + (mul(high, k3[1]) + mul(low, k3[0]))
            for z in range(GZ):
                for v in range(nv):
                    piece = c[v * rank + z * sloc : v * rank + (z + 1) * sloc]
                    core[k, z, v, 2 * j] = piece[:, 0:LANES]
                    core[k, z, v, 2 * j + 1] = piece[:, LANES:]

    def gz_copies(k):
        out = []
        for d in range(1, GZ):
            peer = lax.rem(gz + d, GZ)
            out.append(
                pltpu.make_async_remote_copy(
                    src_ref=core.at[k, peer], dst_ref=rgz.at[k, d - 1],
                    send_sem=zs.at[k, d - 1], recv_sem=zr.at[k, d - 1],
                    device_id=(gx, gy, peer), device_id_type=MESH,
                )
            )
        return out

    def gy_copies(k):
        out = []
        for d in range(1, GY):
            peer = lax.rem(gy + d, GY)
            out.append(
                pltpu.make_async_remote_copy(
                    src_ref=half.at[k, peer], dst_ref=rgy.at[k, d - 1],
                    send_sem=ys.at[k, d - 1], recv_sem=yr.at[k, d - 1],
                    device_id=(gx, peer, gz), device_id_type=MESH,
                )
            )
        return out

    upper = lax.rem(gx + 1, GX)
    across = lax.rem(gx + 2, GX)
    hcols = cols // 2
    sent = pl.multiple_of((across // 2) * hcols, LANES)
    mine = pl.multiple_of((gx // 2) * hcols, LANES)

    def gx_copies(k):
        r = pl.ds(k * step, step)
        return [
            pltpu.make_async_remote_copy(
                src_ref=proj.at[r], dst_ref=q1.at[r],
                send_sem=as_.at[k], recv_sem=ar.at[k],
                device_id=(upper, gy, gz), device_id_type=MESH,
            ),
            pltpu.make_async_remote_copy(
                src_ref=proj.at[r, pl.ds(sent, hcols)], dst_ref=q2.at[r],
                send_sem=bs.at[k], recv_sem=br.at[k],
                device_id=(across, gy, gz), device_id_type=MESH,
            ),
        ]

    zc = [gz_copies(k) for k in range(CHUNKS)]
    yc = [gy_copies(k) for k in range(CHUNKS)]
    xc = [gx_copies(k) for k in range(CHUNKS)]

    def stage_a(k):
        loads[k].wait()
        contract(k)
        if k == 0:
            pl.semaphore_wait(barrier, nr - 1 + GX - 1)
        for c in zc[k]:
            c.start()

    def stage_b(k):
        for c in zc[k]:
            c.wait_recv()

        @pl.loop(0, nv)
        def _(v):
            total = core[k, gz, v]
            for d in range(GZ - 1):
                total = total + rgz[k, d, v]
            half[k, v] = total

        for c in yc[k]:
            c.start()

    def stage_c(k):
        for c in yc[k]:
            c.wait_recv()
        total = half[k, gy]
        for d in range(GY - 1):
            total = total + rgy[k, d]
        xbuf[...] = total.reshape(pairs * sloc, LANES)
        lane = lax.broadcasted_iota(jnp.int32, (pairs, LANES), 1)
        first = lane < tdim
        for p in range(sloc // 2):
            a = xbuf[pl.ds(2 * p, pairs, stride=sloc), :]
            b = xbuf[pl.ds(2 * p + 1, pairs, stride=sloc), :]
            at = pl.ds(p * LANES, LANES)
            proj[pl.ds(k * step, pairs), at] = jnp.where(first, a, pltpu.roll(b, tdim, 1))
            proj[pl.ds(k * step + pairs, pairs), at] = jnp.where(
                first, pltpu.roll(a, tdim, 1), b
            )
        for c in xc[k]:
            c.start()

    stage_a(0)
    stage_a(1)
    stage_b(0)
    stage_a(2)
    stage_b(1)
    stage_a(3)
    stage_b(2)
    stage_b(3)
    for k in range(CHUNKS):
        stage_c(k)

    ph, pw = split(proj[...])
    hh, hw = split(proj[:, pl.ds(mine, hcols)])
    diag = mul_t(ph, ph) + (mul_t(ph, pw) + mul_t(pw, ph))
    for k in range(CHUNKS):
        for c in xc[k]:
            c.wait_recv()
    qh, qw = split(q1[...])
    n1 = mul_t(ph, qh) + (mul_t(ph, qw) + mul_t(pw, qh))
    n1t = mul_t(qh, ph) + (mul_t(qw, ph) + mul_t(qh, pw))
    qh, qw = split(q2[...])
    n2 = mul_t(hh, qh) + (mul_t(hh, qw) + mul_t(hw, qh))
    n2t = mul_t(qh, hh) + (mul_t(qw, hh) + mul_t(qh, hw))
    tbuf[...] = jnp.concatenate([n1t, n2t], axis=1)
    lower = lax.rem(gx + GX - 1, GX)
    swaps = [
        pltpu.make_async_remote_copy(
            src_ref=tbuf, dst_ref=t1, send_sem=ts.at[0], recv_sem=tr.at[0],
            device_id=(lower, gy, gz), device_id_type=MESH,
        ),
        pltpu.make_async_remote_copy(
            src_ref=tbuf, dst_ref=t2, send_sem=ts.at[1], recv_sem=tr.at[1],
            device_id=(across, gy, gz), device_id_type=MESH,
        ),
    ]
    for c in swaps:
        c.start()
    for c in swaps:
        c.wait_recv()
    r1 = t1[:, 0:rows]
    n2 = n2 + t2[:, rows:]
    blocks = []
    for j in range(GX):
        d = lax.rem(j - gx + GX, GX)
        blocks.append(
            jnp.where(d == 0, diag, jnp.where(d == 1, r1, jnp.where(d == 2, n2, n1)))
        )
    whole = jnp.concatenate(blocks, axis=1) * F32(1.0 / (nv * rank * tdim))
    for r in range(nr):
        gp[r] = whole[r * slab : (r + 1) * slab]
    gather = []
    for d in range(1, nr):
        other, where = layer(d)
        gather.append(
            pltpu.make_async_remote_copy(
                src_ref=gp.at[other], dst_ref=rg.at[d - 1],
                send_sem=gs.at[d - 1], recv_sem=gr.at[d - 1],
                device_id=where, device_id_type=MESH,
            )
        )
    for c in gather:
        c.start()
    for c in gather:
        c.wait_recv()
    total = gp[me]
    for d in range(nr - 1):
        total = total + rg[d]
    fin[me] = total
    spread = []
    for d in range(1, nr):
        other, where = layer(d)
        spread.append(
            pltpu.make_async_remote_copy(
                src_ref=fin.at[me], dst_ref=fin.at[me],
                send_sem=hs.at[d - 1], recv_sem=hr.at[d - 1],
                device_id=where, device_id_type=MESH,
            )
        )
    for c in spread:
        c.start()
    for c in spread:
        c.wait_recv()
    for r in range(nr):
        gram[r * slab : (r + 1) * slab, :] = fin[r]
    for group in zc + yc + xc + [swaps, gather, spread]:
        for c in group:
            c.wait_send()


def body(gsize, field, basis_two, basis_three):
    nv, rows, depth, width = field.shape
    rank, tdim = basis_two.shape[1], basis_three.shape[1]
    GX, GY, GZ = gsize
    assert GX == 4 and GY == nv and 4 * depth == 256 and 2 * tdim == LANES
    sloc = rank // GZ
    cols = sloc * tdim
    step = rows // CHUNKS
    pairs = step // 2
    nr = GY * GZ
    slab = rows // nr
    dma = pltpu.SemaphoreType.DMA
    vmem = pl.BlockSpec(memory_space=pltpu.VMEM)
    return pl.pallas_call(
        functools.partial(kernel, field.shape, gsize),
        out_shape=(
            jax.ShapeDtypeStruct((rows, cols), F32),
            jax.ShapeDtypeStruct((rows, GX * rows), F32),
        ),
        in_specs=[pl.BlockSpec(memory_space=pl.ANY), vmem, vmem],
        out_specs=(vmem, vmem),
        scratch_shapes=[
            pltpu.VMEM(field.shape, F32),
            pltpu.VMEM((2 * rank, width), BF16),
            pltpu.VMEM((2, 4 * depth, 4 * tdim), BF16),
            pltpu.VMEM((4 * depth, 4 * tdim), F32),
            pltpu.VMEM((CHUNKS, GZ, nv, pairs, sloc, LANES), F32),
            pltpu.VMEM((CHUNKS, GZ - 1, nv, pairs, sloc, LANES), F32),
            pltpu.VMEM((CHUNKS, nv, pairs, sloc, LANES), F32),
            pltpu.VMEM((CHUNKS, GY - 1, pairs, sloc, LANES), F32),
            pltpu.VMEM((pairs * sloc, LANES), F32),
            pltpu.VMEM((rows, cols), F32),
            pltpu.VMEM((rows, cols // 2), F32),
            pltpu.VMEM((rows, 2 * rows), F32),
            pltpu.VMEM((rows, 2 * rows), F32),
            pltpu.VMEM((rows, 2 * rows), F32),
            pltpu.VMEM((nr, slab, GX * rows), F32),
            pltpu.VMEM((nr - 1, slab, GX * rows), F32),
            pltpu.VMEM((nr, slab, GX * rows), F32),
            dma((CHUNKS,)),
            dma((CHUNKS, GZ - 1)),
            dma((CHUNKS, GZ - 1)),
            dma((CHUNKS, GY - 1)),
            dma((CHUNKS, GY - 1)),
            dma((CHUNKS,)),
            dma((CHUNKS,)),
            dma((CHUNKS,)),
            dma((CHUNKS,)),
            dma((2,)),
            dma((2,)),
            dma((nr - 1,)),
            dma((nr - 1,)),
            dma((nr - 1,)),
            dma((nr - 1,)),
        ],
        compiler_params=pltpu.CompilerParams(
            collective_id=0, has_side_effects=True, vmem_limit_bytes=56 * 2**20
        ),
    )(field, basis_two, basis_three)


def solution(mesh):
    placed = (P(None, "gx", "gz", "gy"), P("gy", None), P("gz", None))
    gsize = tuple(mesh.shape[name] for name in ("gx", "gy", "gz"))
    return jax.shard_map(
        functools.partial(body, gsize),
        mesh=mesh,
        in_specs=placed,
        out_specs=(P("gx", ("gy", "gz")), P("gx", None)),
        check_vma=False,
    )
```

```python
import functools

import jax
import jax.numpy as jnp
from jax import lax
from jax.experimental import pallas as pl
from jax.experimental.pallas import tpu as pltpu
from jax.sharding import PartitionSpec as P

MESH = pl.DeviceIdType.MESH
F32 = jnp.float32
BF16 = jnp.bfloat16
CHUNKS = 8
LAG = 3
LANES = 128


def split(x):
    high = x.astype(BF16)
    return high, (x - high.astype(F32)).astype(BF16)


def mul(a, b):
    return lax.dot_general(a, b, (((1,), (0,)), ((), ())), preferred_element_type=F32)


def mul_t(a, b):
    return lax.dot_general(a, b, (((1,), (1,)), ((), ())), preferred_element_type=F32)


def kernel(shape, gsize, field, b2_ref, b3_ref, proj, gram, *scratch):
    (fbuf, w2, k3, k3f, core, rgz, half, rgy, xbuf, q1, q2, tbuf, t1, t2, gp, rg, fin,
     fsem, zs, zr, ys, yr, as_, ar, bs, br, ts, tr, gs, gr, hs, hr) = scratch
    nv, rows, depth, width = shape
    GX, GY, GZ = gsize
    rank = b2_ref.shape[0]
    tdim = b3_ref.shape[1]
    step = rows // CHUNKS
    pairs = step // 2
    sloc = rank // GZ
    cols = sloc * tdim
    nr = GY * GZ
    slab = rows // nr
    gx, gy, gz = lax.axis_index("gx"), lax.axis_index("gy"), lax.axis_index("gz")
    me = gy * GZ + gz

    def layer(d):
        other = lax.rem(me + d, nr)
        return other, (gx, other // GZ, lax.rem(other, GZ))

    loads = [
        pltpu.make_async_copy(
            field.at[:, pl.ds(k * step, step)], fbuf.at[:, pl.ds(k * step, step)], fsem.at[k]
        )
        for k in range(CHUNKS)
    ]
    for load in loads:
        load.start()

    barrier = pltpu.get_barrier_semaphore()
    for d in range(1, nr):
        pl.semaphore_signal(barrier, inc=1, device_id=layer(d)[1], device_id_type=MESH)
    for d in range(1, GX):
        pl.semaphore_signal(
            barrier, inc=1, device_id=(lax.rem(gx + d, GX), gy, gz), device_id_type=MESH
        )

    high, low = split(b2_ref[...])
    w2[0:rank, :] = high
    w2[rank : 2 * rank, :] = low
    k3f[...] = jnp.zeros_like(k3f)
    for i in range(4):
        k3f[i * depth : (i + 1) * depth, i * tdim : (i + 1) * tdim] = b3_ref[...]
    high, low = split(k3f[...])
    k3[0] = high
    k3[1] = low

    def contract(k):
        @pl.loop(0, pairs // 2, unroll=True)
        def _(j):
            base = k * step + 2 * j
            parts = []
            for v in range(nv):
                tile = jnp.concatenate(
                    [fbuf[v, base + o] for o in (0, pairs, 1, pairs + 1)], axis=0
                )
                high, low = split(tile)
                one = mul_t(w2[...], high)
                two = mul_t(w2[0:rank, :], low)
                parts.append(one[0:rank] + one[rank:] + two)
            high, low = split(jnp.concatenate(parts, axis=0))
            c = mul(high, k3[0]) + (mul(high, k3[1]) + mul(low, k3[0]))
            for z in range(GZ):
                for v in range(nv):
                    piece = c[v * rank + z * sloc : v * rank + (z + 1) * sloc]
                    core[k, z, v, 2 * j] = piece[:, 0:LANES]
                    core[k, z, v, 2 * j + 1] = piece[:, LANES:]

    def gz_copies(k):
        out = []
        for d in range(1, GZ):
            peer = lax.rem(gz + d, GZ)
            out.append(
                pltpu.make_async_remote_copy(
                    src_ref=core.at[k, peer], dst_ref=rgz.at[k, d - 1],
                    send_sem=zs.at[k, d - 1], recv_sem=zr.at[k, d - 1],
                    device_id=(gx, gy, peer), device_id_type=MESH,
                )
            )
        return out

    def gy_copies(k):
        out = []
        for d in range(1, GY):
            peer = lax.rem(gy + d, GY)
            out.append(
                pltpu.make_async_remote_copy(
                    src_ref=half.at[k, peer], dst_ref=rgy.at[k, d - 1],
                    send_sem=ys.at[k, d - 1], recv_sem=yr.at[k, d - 1],
                    device_id=(gx, peer, gz), device_id_type=MESH,
                )
            )
        return out

    upper = lax.rem(gx + 1, GX)
    across = lax.rem(gx + 2, GX)
    hcols = cols // 2
    sent = pl.multiple_of((across // 2) * hcols, LANES)
    mine = pl.multiple_of((gx // 2) * hcols, LANES)

    def gx_copies(k):
        r = pl.ds(k * step, step)
        return [
            pltpu.make_async_remote_copy(
                src_ref=proj.at[r], dst_ref=q1.at[r],
                send_sem=as_.at[k], recv_sem=ar.at[k],
                device_id=(upper, gy, gz), device_id_type=MESH,
            ),
            pltpu.make_async_remote_copy(
                src_ref=proj.at[r, pl.ds(sent, hcols)], dst_ref=q2.at[r],
                send_sem=bs.at[k], recv_sem=br.at[k],
                device_id=(across, gy, gz), device_id_type=MESH,
            ),
        ]

    zc = [gz_copies(k) for k in range(CHUNKS)]
    yc = [gy_copies(k) for k in range(CHUNKS)]
    xc = [gx_copies(k) for k in range(CHUNKS)]

    def stage_a(k):
        loads[k].wait()
        contract(k)
        if k == 0:
            pl.semaphore_wait(barrier, nr - 1 + GX - 1)
        for c in zc[k]:
            c.start()

    def stage_b(k):
        for c in zc[k]:
            c.wait_recv()

        @pl.loop(0, nv)
        def _(v):
            total = core[k, gz, v]
            for d in range(GZ - 1):
                total = total + rgz[k, d, v]
            half[k, v] = total

        for c in yc[k]:
            c.start()

    def stage_c(k):
        for c in yc[k]:
            c.wait_recv()
        total = half[k, gy]
        for d in range(GY - 1):
            total = total + rgy[k, d]
        xbuf[...] = total.reshape(pairs * sloc, LANES)
        lane = lax.broadcasted_iota(jnp.int32, (pairs, LANES), 1)
        first = lane < tdim
        for p in range(sloc // 2):
            a = xbuf[pl.ds(2 * p, pairs, stride=sloc), :]
            b = xbuf[pl.ds(2 * p + 1, pairs, stride=sloc), :]
            at = pl.ds(p * LANES, LANES)
            proj[pl.ds(k * step, pairs), at] = jnp.where(first, a, pltpu.roll(b, tdim, 1))
            proj[pl.ds(k * step + pairs, pairs), at] = jnp.where(
                first, pltpu.roll(a, tdim, 1), b
            )
        for c in xc[k]:
            c.start()

    for k in range(CHUNKS + LAG):
        if k < CHUNKS:
            stage_a(k)
        if 1 <= k <= CHUNKS:
            stage_b(k - 1)
        if k >= LAG:
            stage_c(k - LAG)

    ph, pw = split(proj[...])
    hh, hw = split(proj[:, pl.ds(mine, hcols)])
    diag = mul_t(ph, ph) + (mul_t(ph, pw) + mul_t(pw, ph))
    for k in range(CHUNKS):
        for c in xc[k]:
            c.wait_recv()
    qh, qw = split(q1[...])
    n1 = mul_t(ph, qh) + (mul_t(ph, qw) + mul_t(pw, qh))
    n1t = mul_t(qh, ph) + (mul_t(qw, ph) + mul_t(qh, pw))
    qh, qw = split(q2[...])
    n2 = mul_t(hh, qh) + (mul_t(hh, qw) + mul_t(hw, qh))
    n2t = mul_t(qh, hh) + (mul_t(qw, hh) + mul_t(qh, hw))
    tbuf[...] = jnp.concatenate([n1t, n2t], axis=1)
    lower = lax.rem(gx + GX - 1, GX)
    swaps = [
        pltpu.make_async_remote_copy(
            src_ref=tbuf, dst_ref=t1, send_sem=ts.at[0], recv_sem=tr.at[0],
            device_id=(lower, gy, gz), device_id_type=MESH,
        ),
        pltpu.make_async_remote_copy(
            src_ref=tbuf, dst_ref=t2, send_sem=ts.at[1], recv_sem=tr.at[1],
            device_id=(across, gy, gz), device_id_type=MESH,
        ),
    ]
    for c in swaps:
        c.start()
    for c in swaps:
        c.wait_recv()
    r1 = t1[:, 0:rows]
    n2 = n2 + t2[:, rows:]
    blocks = []
    for j in range(GX):
        d = lax.rem(j - gx + GX, GX)
        blocks.append(
            jnp.where(d == 0, diag, jnp.where(d == 1, r1, jnp.where(d == 2, n2, n1)))
        )
    whole = jnp.concatenate(blocks, axis=1) * F32(1.0 / (nv * rank * tdim))
    for r in range(nr):
        gp[r] = whole[r * slab : (r + 1) * slab]
    gather = []
    for d in range(1, nr):
        other, where = layer(d)
        gather.append(
            pltpu.make_async_remote_copy(
                src_ref=gp.at[other], dst_ref=rg.at[d - 1],
                send_sem=gs.at[d - 1], recv_sem=gr.at[d - 1],
                device_id=where, device_id_type=MESH,
            )
        )
    for c in gather:
        c.start()
    for c in gather:
        c.wait_recv()
    total = gp[me]
    for d in range(nr - 1):
        total = total + rg[d]
    fin[me] = total
    spread = []
    for d in range(1, nr):
        other, where = layer(d)
        spread.append(
            pltpu.make_async_remote_copy(
                src_ref=fin.at[me], dst_ref=fin.at[me],
                send_sem=hs.at[d - 1], recv_sem=hr.at[d - 1],
                device_id=where, device_id_type=MESH,
            )
        )
    for c in spread:
        c.start()
    for c in spread:
        c.wait_recv()
    for r in range(nr):
        gram[r * slab : (r + 1) * slab, :] = fin[r]
    for group in zc + yc + xc + [swaps, gather, spread]:
        for c in group:
            c.wait_send()


def body(gsize, field, basis_two, basis_three):
    nv, rows, depth, width = field.shape
    rank, tdim = basis_two.shape[1], basis_three.shape[1]
    GX, GY, GZ = gsize
    assert GX == 4 and GY == nv and 4 * depth == 256 and 2 * tdim == LANES
    sloc = rank // GZ
    cols = sloc * tdim
    step = rows // CHUNKS
    pairs = step // 2
    nr = GY * GZ
    slab = rows // nr
    dma = pltpu.SemaphoreType.DMA
    vmem = pl.BlockSpec(memory_space=pltpu.VMEM)
    return pl.pallas_call(
        functools.partial(kernel, field.shape, gsize),
        out_shape=(
            jax.ShapeDtypeStruct((rows, cols), F32),
            jax.ShapeDtypeStruct((rows, GX * rows), F32),
        ),
        in_specs=[pl.BlockSpec(memory_space=pl.ANY), vmem, vmem],
        out_specs=(vmem, vmem),
        scratch_shapes=[
            pltpu.VMEM(field.shape, F32),
            pltpu.VMEM((2 * rank, width), BF16),
            pltpu.VMEM((2, 4 * depth, 4 * tdim), BF16),
            pltpu.VMEM((4 * depth, 4 * tdim), F32),
            pltpu.VMEM((CHUNKS, GZ, nv, pairs, sloc, LANES), F32),
            pltpu.VMEM((CHUNKS, GZ - 1, nv, pairs, sloc, LANES), F32),
            pltpu.VMEM((CHUNKS, nv, pairs, sloc, LANES), F32),
            pltpu.VMEM((CHUNKS, GY - 1, pairs, sloc, LANES), F32),
            pltpu.VMEM((pairs * sloc, LANES), F32),
            pltpu.VMEM((rows, cols), F32),
            pltpu.VMEM((rows, cols // 2), F32),
            pltpu.VMEM((rows, 2 * rows), F32),
            pltpu.VMEM((rows, 2 * rows), F32),
            pltpu.VMEM((rows, 2 * rows), F32),
            pltpu.VMEM((nr, slab, GX * rows), F32),
            pltpu.VMEM((nr - 1, slab, GX * rows), F32),
            pltpu.VMEM((nr, slab, GX * rows), F32),
            dma((CHUNKS,)),
            dma((CHUNKS, GZ - 1)),
            dma((CHUNKS, GZ - 1)),
            dma((CHUNKS, GY - 1)),
            dma((CHUNKS, GY - 1)),
            dma((CHUNKS,)),
            dma((CHUNKS,)),
            dma((CHUNKS,)),
            dma((CHUNKS,)),
            dma((2,)),
            dma((2,)),
            dma((nr - 1,)),
            dma((nr - 1,)),
            dma((nr - 1,)),
            dma((nr - 1,)),
        ],
        compiler_params=pltpu.CompilerParams(
            collective_id=0, has_side_effects=True, vmem_limit_bytes=56 * 2**20
        ),
    )(field, basis_two.T, basis_three)


def solution(mesh):
    placed = (P(None, "gx", "gz", "gy"), P("gy", None), P("gz", None))
    gsize = tuple(mesh.shape[name] for name in ("gx", "gy", "gz"))
    return jax.shard_map(
        functools.partial(body, gsize),
        mesh=mesh,
        in_specs=placed,
        out_specs=(P("gx", ("gy", "gz")), P("gx", None)),
        check_vma=False,
    )
```

```python
import functools

import jax
import jax.numpy as jnp
from jax import lax
from jax.experimental import pallas as pl
from jax.experimental.pallas import tpu as pltpu
from jax.sharding import PartitionSpec as P

MESH = pl.DeviceIdType.MESH
F32 = jnp.float32
BF16 = jnp.bfloat16
CHUNKS = 8
LAG = 3
LANES = 128


def split(x):
    high = x.astype(BF16)
    return high, (x - high.astype(F32)).astype(BF16)


def mul(a, b):
    return lax.dot_general(a, b, (((1,), (0,)), ((), ())), preferred_element_type=F32)


def mul_t(a, b):
    return lax.dot_general(a, b, (((1,), (1,)), ((), ())), preferred_element_type=F32)


def kernel(shape, gsize, field, b2_ref, b3_ref, proj, gram, *scratch):
    (fbuf, w2f, w2, k3, k3f, core, rgz, half, rgy, xbuf, q1, q2, tbuf, t1, t2, gp, rg, fin,
     fsem, zs, zr, ys, yr, as_, ar, bs, br, ts, tr, gs, gr, hs, hr) = scratch
    nv, rows, depth, width = shape
    GX, GY, GZ = gsize
    rank = b2_ref.shape[0]
    tdim = b3_ref.shape[1]
    step = rows // CHUNKS
    pairs = step // 2
    sloc = rank // GZ
    cols = sloc * tdim
    nr = GY * GZ
    slab = rows // nr
    gx, gy, gz = lax.axis_index("gx"), lax.axis_index("gy"), lax.axis_index("gz")
    me = gy * GZ + gz

    def layer(d):
        other = lax.rem(me + d, nr)
        return other, (gx, other // GZ, lax.rem(other, GZ))

    loads = [
        pltpu.make_async_copy(
            field.at[:, pl.ds(k * step, step)], fbuf.at[:, pl.ds(k * step, step)], fsem.at[k]
        )
        for k in range(CHUNKS)
    ]
    for load in loads:
        load.start()

    barrier = pltpu.get_barrier_semaphore()
    for d in range(1, nr):
        pl.semaphore_signal(barrier, inc=1, device_id=layer(d)[1], device_id_type=MESH)
    for d in range(1, GX):
        pl.semaphore_signal(
            barrier, inc=1, device_id=(lax.rem(gx + d, GX), gy, gz), device_id_type=MESH
        )

    turned = b2_ref[...].T
    w2f[...] = jnp.zeros_like(w2f)
    for z in range(GZ):
        for v in range(nv):
            at = (z * nv + v) * sloc
            w2f[v * width : (v + 1) * width, at : at + sloc] = turned[
                :, z * sloc : (z + 1) * sloc
            ]
    high, low = split(w2f[...])
    w2[0] = high
    w2[1] = low
    k3f[...] = jnp.zeros_like(k3f)
    turned = b3_ref[...].T
    for i in range(4):
        k3f[i * tdim : (i + 1) * tdim, i * depth : (i + 1) * depth] = turned
    high, low = split(k3f[...])
    k3[0 : 4 * tdim] = high
    k3[4 * tdim :] = low

    def contract(k):
        parts = [
            split(fbuf[v, k * step : (k + 1) * step].reshape(step * depth, width))
            for v in range(nv)
        ]
        high = jnp.concatenate([h for h, _ in parts], axis=1)
        low = jnp.concatenate([l for _, l in parts], axis=1)
        first = mul(high, w2[0]) + (mul(high, w2[1]) + mul(low, w2[0]))
        high, low = split(first)
        for j in range(pairs // 2):
            order = (2 * j, 2 * j + pairs, 2 * j + 1, 2 * j + 1 + pairs)
            h = jnp.concatenate([high[a * depth : (a + 1) * depth] for a in order], axis=0)
            l = jnp.concatenate([low[a * depth : (a + 1) * depth] for a in order], axis=0)
            one = mul(k3[...], h)
            two = mul(k3[0 : 4 * tdim], l)
            c = one[0 : 4 * tdim] + (one[4 * tdim :] + two)
            for z in range(GZ):
                core[k, z, j * 4 * tdim : (j + 1) * 4 * tdim] = c[
                    :, z * nv * sloc : (z + 1) * nv * sloc
                ]

    def gz_copies(k):
        out = []
        for d in range(1, GZ):
            peer = lax.rem(gz + d, GZ)
            out.append(
                pltpu.make_async_remote_copy(
                    src_ref=core.at[k, peer], dst_ref=rgz.at[k, d - 1],
                    send_sem=zs.at[k, d - 1], recv_sem=zr.at[k, d - 1],
                    device_id=(gx, gy, peer), device_id_type=MESH,
                )
            )
        return out

    def gy_copies(k):
        out = []
        for d in range(1, GY):
            peer = lax.rem(gy + d, GY)
            out.append(
                pltpu.make_async_remote_copy(
                    src_ref=half.at[k, peer], dst_ref=rgy.at[k, d - 1],
                    send_sem=ys.at[k, d - 1], recv_sem=yr.at[k, d - 1],
                    device_id=(gx, peer, gz), device_id_type=MESH,
                )
            )
        return out

    upper = lax.rem(gx + 1, GX)
    across = lax.rem(gx + 2, GX)
    hcols = cols // 2
    sent = pl.multiple_of((across // 2) * hcols, LANES)
    mine = pl.multiple_of((gx // 2) * hcols, LANES)

    def gx_copies(k):
        r = pl.ds(k * step, step)
        return [
            pltpu.make_async_remote_copy(
                src_ref=proj.at[r], dst_ref=q1.at[r],
                send_sem=as_.at[k], recv_sem=ar.at[k],
                device_id=(upper, gy, gz), device_id_type=MESH,
            ),
            pltpu.make_async_remote_copy(
                src_ref=proj.at[r, pl.ds(sent, hcols)], dst_ref=q2.at[r],
                send_sem=bs.at[k], recv_sem=br.at[k],
                device_id=(across, gy, gz), device_id_type=MESH,
            ),
        ]

    zc = [gz_copies(k) for k in range(CHUNKS)]
    yc = [gy_copies(k) for k in range(CHUNKS)]
    xc = [gx_copies(k) for k in range(CHUNKS)]

    def stage_a(k):
        loads[k].wait()
        contract(k)
        if k == 0:
            pl.semaphore_wait(barrier, nr - 1 + GX - 1)
        for c in zc[k]:
            c.start()

    def stage_b(k):
        for c in zc[k]:
            c.wait_recv()

        total = core[k, gz]
        for d in range(GZ - 1):
            total = total + rgz[k, d]
        for q in range(pairs):
            t = total[q * LANES : (q + 1) * LANES].T
            for v in range(nv):
                half[k, v, q] = t[v * sloc : (v + 1) * sloc]

        for c in yc[k]:
            c.start()

    def stage_c(k):
        for c in yc[k]:
            c.wait_recv()
        total = half[k, gy]
        for d in range(GY - 1):
            total = total + rgy[k, d]
        xbuf[...] = total.reshape(pairs * sloc, LANES)
        lane = lax.broadcasted_iota(jnp.int32, (pairs, LANES), 1)
        first = lane < tdim
        for p in range(sloc // 2):
            a = xbuf[pl.ds(2 * p, pairs, stride=sloc), :]
            b = xbuf[pl.ds(2 * p + 1, pairs, stride=sloc), :]
            at = pl.ds(p * LANES, LANES)
            proj[pl.ds(k * step, pairs), at] = jnp.where(first, a, pltpu.roll(b, tdim, 1))
            proj[pl.ds(k * step + pairs, pairs), at] = jnp.where(
                first, pltpu.roll(a, tdim, 1), b
            )
        for c in xc[k]:
            c.start()

    for k in range(CHUNKS + LAG):
        if k < CHUNKS:
            stage_a(k)
        if 1 <= k <= CHUNKS:
            stage_b(k - 1)
        if k >= LAG:
            stage_c(k - LAG)

    ph, pw = split(proj[...])
    hh, hw = split(proj[:, pl.ds(mine, hcols)])
    diag = mul_t(ph, ph) + (mul_t(ph, pw) + mul_t(pw, ph))
    for k in range(CHUNKS):
        for c in xc[k]:
            c.wait_recv()
    qh, qw = split(q1[...])
    n1 = mul_t(ph, qh) + (mul_t(ph, qw) + mul_t(pw, qh))
    n1t = mul_t(qh, ph) + (mul_t(qw, ph) + mul_t(qh, pw))
    qh, qw = split(q2[...])
    n2 = mul_t(hh, qh) + (mul_t(hh, qw) + mul_t(hw, qh))
    n2t = mul_t(qh, hh) + (mul_t(qw, hh) + mul_t(qh, hw))
    tbuf[...] = jnp.concatenate([n1t, n2t], axis=1)
    lower = lax.rem(gx + GX - 1, GX)
    swaps = [
        pltpu.make_async_remote_copy(
            src_ref=tbuf, dst_ref=t1, send_sem=ts.at[0], recv_sem=tr.at[0],
            device_id=(lower, gy, gz), device_id_type=MESH,
        ),
        pltpu.make_async_remote_copy(
            src_ref=tbuf, dst_ref=t2, send_sem=ts.at[1], recv_sem=tr.at[1],
            device_id=(across, gy, gz), device_id_type=MESH,
        ),
    ]
    for c in swaps:
        c.start()
    for c in swaps:
        c.wait_recv()
    r1 = t1[:, 0:rows]
    n2 = n2 + t2[:, rows:]
    blocks = []
    for j in range(GX):
        d = lax.rem(j - gx + GX, GX)
        blocks.append(
            jnp.where(d == 0, diag, jnp.where(d == 1, r1, jnp.where(d == 2, n2, n1)))
        )
    whole = jnp.concatenate(blocks, axis=1) * F32(1.0 / (nv * rank * tdim))
    for r in range(nr):
        gp[r] = whole[r * slab : (r + 1) * slab]
    gather = []
    for d in range(1, nr):
        other, where = layer(d)
        gather.append(
            pltpu.make_async_remote_copy(
                src_ref=gp.at[other], dst_ref=rg.at[d - 1],
                send_sem=gs.at[d - 1], recv_sem=gr.at[d - 1],
                device_id=where, device_id_type=MESH,
            )
        )
    for c in gather:
        c.start()
    for c in gather:
        c.wait_recv()
    total = gp[me]
    for d in range(nr - 1):
        total = total + rg[d]
    fin[me] = total
    spread = []
    for d in range(1, nr):
        other, where = layer(d)
        spread.append(
            pltpu.make_async_remote_copy(
                src_ref=fin.at[me], dst_ref=fin.at[me],
                send_sem=hs.at[d - 1], recv_sem=hr.at[d - 1],
                device_id=where, device_id_type=MESH,
            )
        )
    for c in spread:
        c.start()
    for c in spread:
        c.wait_recv()
    for r in range(nr):
        gram[r * slab : (r + 1) * slab, :] = fin[r]
    for group in zc + yc + xc + [swaps, gather, spread]:
        for c in group:
            c.wait_send()


def body(gsize, field, basis_two, basis_three):
    nv, rows, depth, width = field.shape
    rank, tdim = basis_two.shape[1], basis_three.shape[1]
    GX, GY, GZ = gsize
    assert GX == 4 and GY == nv and 4 * depth == 256 and 2 * tdim == LANES
    sloc = rank // GZ
    cols = sloc * tdim
    step = rows // CHUNKS
    pairs = step // 2
    nr = GY * GZ
    slab = rows // nr
    dma = pltpu.SemaphoreType.DMA
    vmem = pl.BlockSpec(memory_space=pltpu.VMEM)
    return pl.pallas_call(
        functools.partial(kernel, field.shape, gsize),
        out_shape=(
            jax.ShapeDtypeStruct((rows, cols), F32),
            jax.ShapeDtypeStruct((rows, GX * rows), F32),
        ),
        in_specs=[pl.BlockSpec(memory_space=pl.ANY), vmem, vmem],
        out_specs=(vmem, vmem),
        scratch_shapes=[
            pltpu.VMEM(field.shape, F32),
            pltpu.VMEM((nv * width, nv * rank), F32),
            pltpu.VMEM((2, nv * width, nv * rank), BF16),
            pltpu.VMEM((8 * tdim, 4 * depth), BF16),
            pltpu.VMEM((4 * tdim, 4 * depth), F32),
            pltpu.VMEM((CHUNKS, GZ, step * tdim, nv * sloc), F32),
            pltpu.VMEM((CHUNKS, GZ - 1, step * tdim, nv * sloc), F32),
            pltpu.VMEM((CHUNKS, nv, pairs, sloc, LANES), F32),
            pltpu.VMEM((CHUNKS, GY - 1, pairs, sloc, LANES), F32),
            pltpu.VMEM((pairs * sloc, LANES), F32),
            pltpu.VMEM((rows, cols), F32),
            pltpu.VMEM((rows, cols // 2), F32),
            pltpu.VMEM((rows, 2 * rows), F32),
            pltpu.VMEM((rows, 2 * rows), F32),
            pltpu.VMEM((rows, 2 * rows), F32),
            pltpu.VMEM((nr, slab, GX * rows), F32),
            pltpu.VMEM((nr - 1, slab, GX * rows), F32),
            pltpu.VMEM((nr, slab, GX * rows), F32),
            dma((CHUNKS,)),
            dma((CHUNKS, GZ - 1)),
            dma((CHUNKS, GZ - 1)),
            dma((CHUNKS, GY - 1)),
            dma((CHUNKS, GY - 1)),
            dma((CHUNKS,)),
            dma((CHUNKS,)),
            dma((CHUNKS,)),
            dma((CHUNKS,)),
            dma((2,)),
            dma((2,)),
            dma((nr - 1,)),
            dma((nr - 1,)),
            dma((nr - 1,)),
            dma((nr - 1,)),
        ],
        compiler_params=pltpu.CompilerParams(
            collective_id=0, has_side_effects=True, vmem_limit_bytes=56 * 2**20
        ),
    )(field, basis_two.T, basis_three)


def solution(mesh):
    placed = (P(None, "gx", "gz", "gy"), P("gy", None), P("gz", None))
    gsize = tuple(mesh.shape[name] for name in ("gx", "gy", "gz"))
    return jax.shard_map(
        functools.partial(body, gsize),
        mesh=mesh,
        in_specs=placed,
        out_specs=(P("gx", ("gy", "gz")), P("gx", None)),
        check_vma=False,
    )
```

```python
import functools

import jax
import jax.numpy as jnp
from jax import lax
from jax.experimental import pallas as pl
from jax.experimental.pallas import tpu as pltpu
from jax.sharding import PartitionSpec as P

MESH = pl.DeviceIdType.MESH
F32 = jnp.float32
BF16 = jnp.bfloat16
CHUNKS = 8
LAG = 3
LANES = 128


def split(x):
    high = x.astype(BF16)
    return high, (x - high.astype(F32)).astype(BF16)


def mul(a, b):
    return lax.dot_general(a, b, (((1,), (0,)), ((), ())), preferred_element_type=F32)


def mul_t(a, b):
    return lax.dot_general(a, b, (((1,), (1,)), ((), ())), preferred_element_type=F32)


def kernel(shape, gsize, field, b2_ref, b3_ref, proj, gram, *scratch):
    (fbuf, w2f, w2, k3, k3f, core, rgz, half, rgy, xbuf, q1, q2, tbuf, t1, t2, gp, rg, fin,
     fsem, zs, zr, ys, yr, as_, ar, bs, br, ts, tr, gs, gr, hs, hr) = scratch
    nv, rows, depth, width = shape
    GX, GY, GZ = gsize
    rank = b2_ref.shape[0]
    tdim = b3_ref.shape[1]
    step = rows // CHUNKS
    pairs = step // 2
    sloc = rank // GZ
    cols = sloc * tdim
    nr = GY * GZ
    slab = rows // nr
    gx, gy, gz = lax.axis_index("gx"), lax.axis_index("gy"), lax.axis_index("gz")
    me = gy * GZ + gz

    def layer(d):
        other = lax.rem(me + d, nr)
        return other, (gx, other // GZ, lax.rem(other, GZ))

    def rows_of(k):
        return pl.ds(pl.multiple_of(k * step, step), step)

    def load(k):
        r = rows_of(k)
        return pltpu.make_async_copy(field.at[:, r], fbuf.at[:, r], fsem.at[k])

    for k in range(CHUNKS):
        load(k).start()

    barrier = pltpu.get_barrier_semaphore()
    for d in range(1, nr):
        pl.semaphore_signal(barrier, inc=1, device_id=layer(d)[1], device_id_type=MESH)
    for d in range(1, GX):
        pl.semaphore_signal(
            barrier, inc=1, device_id=(lax.rem(gx + d, GX), gy, gz), device_id_type=MESH
        )

    turned = b2_ref[...].T
    w2f[...] = jnp.zeros_like(w2f)
    for z in range(GZ):
        for v in range(nv):
            at = (z * nv + v) * sloc
            w2f[v * width : (v + 1) * width, at : at + sloc] = turned[
                :, z * sloc : (z + 1) * sloc
            ]
    high, low = split(w2f[...])
    w2[0] = high
    w2[1] = low
    k3f[...] = jnp.zeros_like(k3f)
    turned = b3_ref[...].T
    for i in range(4):
        k3f[i * tdim : (i + 1) * tdim, i * depth : (i + 1) * depth] = turned
    high, low = split(k3f[...])
    k3[0 : 4 * tdim] = high
    k3[4 * tdim :] = low

    def contract(k):
        parts = [
            split(fbuf[v, rows_of(k)].reshape(step * depth, width))
            for v in range(nv)
        ]
        high = jnp.concatenate([h for h, _ in parts], axis=1)
        low = jnp.concatenate([l for _, l in parts], axis=1)
        first = mul(high, w2[0]) + (mul(high, w2[1]) + mul(low, w2[0]))
        high, low = split(first)
        for j in range(pairs // 2):
            order = (2 * j, 2 * j + pairs, 2 * j + 1, 2 * j + 1 + pairs)
            h = jnp.concatenate([high[a * depth : (a + 1) * depth] for a in order], axis=0)
            l = jnp.concatenate([low[a * depth : (a + 1) * depth] for a in order], axis=0)
            one = mul(k3[...], h)
            two = mul(k3[0 : 4 * tdim], l)
            c = one[0 : 4 * tdim] + (one[4 * tdim :] + two)
            for z in range(GZ):
                core[k, z, j * 4 * tdim : (j + 1) * 4 * tdim] = c[
                    :, z * nv * sloc : (z + 1) * nv * sloc
                ]

    def gz_copies(k):
        out = []
        for d in range(1, GZ):
            peer = lax.rem(gz + d, GZ)
            out.append(
                pltpu.make_async_remote_copy(
                    src_ref=core.at[k, peer], dst_ref=rgz.at[k, d - 1],
                    send_sem=zs.at[k, d - 1], recv_sem=zr.at[k, d - 1],
                    device_id=(gx, gy, peer), device_id_type=MESH,
                )
            )
        return out

    def gy_copies(k):
        out = []
        for d in range(1, GY):
            peer = lax.rem(gy + d, GY)
            out.append(
                pltpu.make_async_remote_copy(
                    src_ref=half.at[k, peer], dst_ref=rgy.at[k, d - 1],
                    send_sem=ys.at[k, d - 1], recv_sem=yr.at[k, d - 1],
                    device_id=(gx, peer, gz), device_id_type=MESH,
                )
            )
        return out

    upper = lax.rem(gx + 1, GX)
    across = lax.rem(gx + 2, GX)
    hcols = cols // 2
    sent = pl.multiple_of((across // 2) * hcols, LANES)
    mine = pl.multiple_of((gx // 2) * hcols, LANES)

    def gx_copies(k):
        r = rows_of(k)
        return [
            pltpu.make_async_remote_copy(
                src_ref=proj.at[r], dst_ref=q1.at[r],
                send_sem=as_.at[k], recv_sem=ar.at[k],
                device_id=(upper, gy, gz), device_id_type=MESH,
            ),
            pltpu.make_async_remote_copy(
                src_ref=proj.at[r, pl.ds(sent, hcols)], dst_ref=q2.at[r],
                send_sem=bs.at[k], recv_sem=br.at[k],
                device_id=(across, gy, gz), device_id_type=MESH,
            ),
        ]

    def stage_a(k):
        load(k).wait()
        contract(k)

        @pl.when(k == 0)
        def _():
            pl.semaphore_wait(barrier, nr - 1 + GX - 1)

        for c in gz_copies(k):
            c.start()

    def stage_b(k):
        for c in gz_copies(k):
            c.wait_recv()
        total = core[k, gz]
        for d in range(GZ - 1):
            total = total + rgz[k, d]
        for q in range(pairs):
            t = total[q * LANES : (q + 1) * LANES].T
            for v in range(nv):
                half[k, v, q] = t[v * sloc : (v + 1) * sloc]
        for c in gy_copies(k):
            c.start()

    def stage_c(k):
        for c in gy_copies(k):
            c.wait_recv()
        total = half[k, gy]
        for d in range(GY - 1):
            total = total + rgy[k, d]
        xbuf[...] = total.reshape(pairs * sloc, LANES)
        lane = lax.broadcasted_iota(jnp.int32, (pairs, LANES), 1)
        first = lane < tdim
        done = []
        for p in range(sloc // 2):
            a = xbuf[pl.ds(2 * p, pairs, stride=sloc), :]
            b = xbuf[pl.ds(2 * p + 1, pairs, stride=sloc), :]
            done.append(
                jnp.concatenate(
                    [
                        jnp.where(first, a, pltpu.roll(b, tdim, 1)),
                        jnp.where(first, pltpu.roll(a, tdim, 1), b),
                    ],
                    axis=0,
                )
            )
        proj[rows_of(k), :] = jnp.concatenate(done, axis=1)
        for c in gx_copies(k):
            c.start()

    @pl.loop(0, CHUNKS + LAG)
    def _(k):
        @pl.when(k < CHUNKS)
        def _():
            stage_a(k)

        @pl.when((k >= 1) & (k <= CHUNKS))
        def _():
            stage_b(k - 1)

        @pl.when(k >= LAG)
        def _():
            stage_c(k - LAG)

    ph, pw = split(proj[...])
    hh, hw = split(proj[:, pl.ds(mine, hcols)])
    diag = mul_t(ph, ph) + (mul_t(ph, pw) + mul_t(pw, ph))

    @pl.loop(0, CHUNKS)
    def _(k):
        for c in gx_copies(k):
            c.wait_recv()

    qh, qw = split(q1[...])
    n1 = mul_t(ph, qh) + (mul_t(ph, qw) + mul_t(pw, qh))
    n1t = mul_t(qh, ph) + (mul_t(qw, ph) + mul_t(qh, pw))
    qh, qw = split(q2[...])
    n2 = mul_t(hh, qh) + (mul_t(hh, qw) + mul_t(hw, qh))
    n2t = mul_t(qh, hh) + (mul_t(qw, hh) + mul_t(qh, hw))
    tbuf[...] = jnp.concatenate([n1t, n2t], axis=1)
    lower = lax.rem(gx + GX - 1, GX)
    swaps = [
        pltpu.make_async_remote_copy(
            src_ref=tbuf, dst_ref=t1, send_sem=ts.at[0], recv_sem=tr.at[0],
            device_id=(lower, gy, gz), device_id_type=MESH,
        ),
        pltpu.make_async_remote_copy(
            src_ref=tbuf, dst_ref=t2, send_sem=ts.at[1], recv_sem=tr.at[1],
            device_id=(across, gy, gz), device_id_type=MESH,
        ),
    ]
    for c in swaps:
        c.start()
    for c in swaps:
        c.wait_recv()
    r1 = t1[:, 0:rows]
    n2 = n2 + t2[:, rows:]
    blocks = []
    for j in range(GX):
        d = lax.rem(j - gx + GX, GX)
        blocks.append(
            jnp.where(d == 0, diag, jnp.where(d == 1, r1, jnp.where(d == 2, n2, n1)))
        )
    whole = jnp.concatenate(blocks, axis=1) * F32(1.0 / (nv * rank * tdim))
    for r in range(nr):
        gp[r] = whole[r * slab : (r + 1) * slab]
    gather = []
    for d in range(1, nr):
        other, where = layer(d)
        gather.append(
            pltpu.make_async_remote_copy(
                src_ref=gp.at[other], dst_ref=rg.at[d - 1],
                send_sem=gs.at[d - 1], recv_sem=gr.at[d - 1],
                device_id=where, device_id_type=MESH,
            )
        )
    for c in gather:
        c.start()
    for c in gather:
        c.wait_recv()
    total = gp[me]
    for d in range(nr - 1):
        total = total + rg[d]
    fin[me] = total
    spread = []
    for d in range(1, nr):
        other, where = layer(d)
        spread.append(
            pltpu.make_async_remote_copy(
                src_ref=fin.at[me], dst_ref=fin.at[me],
                send_sem=hs.at[d - 1], recv_sem=hr.at[d - 1],
                device_id=where, device_id_type=MESH,
            )
        )
    for c in spread:
        c.start()
    for c in spread:
        c.wait_recv()
    for r in range(nr):
        gram[r * slab : (r + 1) * slab, :] = fin[r]
    for c in swaps + gather + spread:
        c.wait_send()

    @pl.loop(0, CHUNKS)
    def _(k):
        for c in gz_copies(k) + gy_copies(k) + gx_copies(k):
            c.wait_send()


def body(gsize, field, basis_two, basis_three):
    nv, rows, depth, width = field.shape
    rank, tdim = basis_two.shape[1], basis_three.shape[1]
    GX, GY, GZ = gsize
    assert GX == 4 and GY == nv and 4 * depth == 256 and 2 * tdim == LANES
    sloc = rank // GZ
    cols = sloc * tdim
    step = rows // CHUNKS
    pairs = step // 2
    nr = GY * GZ
    slab = rows // nr
    dma = pltpu.SemaphoreType.DMA
    vmem = pl.BlockSpec(memory_space=pltpu.VMEM)
    return pl.pallas_call(
        functools.partial(kernel, field.shape, gsize),
        out_shape=(
            jax.ShapeDtypeStruct((rows, cols), F32),
            jax.ShapeDtypeStruct((rows, GX * rows), F32),
        ),
        in_specs=[pl.BlockSpec(memory_space=pl.ANY), vmem, vmem],
        out_specs=(vmem, vmem),
        scratch_shapes=[
            pltpu.VMEM(field.shape, F32),
            pltpu.VMEM((nv * width, nv * rank), F32),
            pltpu.VMEM((2, nv * width, nv * rank), BF16),
            pltpu.VMEM((8 * tdim, 4 * depth), BF16),
            pltpu.VMEM((4 * tdim, 4 * depth), F32),
            pltpu.VMEM((CHUNKS, GZ, step * tdim, nv * sloc), F32),
            pltpu.VMEM((CHUNKS, GZ - 1, step * tdim, nv * sloc), F32),
            pltpu.VMEM((CHUNKS, nv, pairs, sloc, LANES), F32),
            pltpu.VMEM((CHUNKS, GY - 1, pairs, sloc, LANES), F32),
            pltpu.VMEM((pairs * sloc, LANES), F32),
            pltpu.VMEM((rows, cols), F32),
            pltpu.VMEM((rows, cols // 2), F32),
            pltpu.VMEM((rows, 2 * rows), F32),
            pltpu.VMEM((rows, 2 * rows), F32),
            pltpu.VMEM((rows, 2 * rows), F32),
            pltpu.VMEM((nr, slab, GX * rows), F32),
            pltpu.VMEM((nr - 1, slab, GX * rows), F32),
            pltpu.VMEM((nr, slab, GX * rows), F32),
            dma((CHUNKS,)),
            dma((CHUNKS, GZ - 1)),
            dma((CHUNKS, GZ - 1)),
            dma((CHUNKS, GY - 1)),
            dma((CHUNKS, GY - 1)),
            dma((CHUNKS,)),
            dma((CHUNKS,)),
            dma((CHUNKS,)),
            dma((CHUNKS,)),
            dma((2,)),
            dma((2,)),
            dma((nr - 1,)),
            dma((nr - 1,)),
            dma((nr - 1,)),
            dma((nr - 1,)),
        ],
        compiler_params=pltpu.CompilerParams(
            collective_id=0, has_side_effects=True, vmem_limit_bytes=56 * 2**20
        ),
    )(field, basis_two.T, basis_three)


def solution(mesh):
    placed = (P(None, "gx", "gz", "gy"), P("gy", None), P("gz", None))
    gsize = tuple(mesh.shape[name] for name in ("gx", "gy", "gz"))
    return jax.shard_map(
        functools.partial(body, gsize),
        mesh=mesh,
        in_specs=placed,
        out_specs=(P("gx", ("gy", "gz")), P("gx", None)),
        check_vma=False,
    )
```

```python
import functools

import jax
import jax.numpy as jnp
from jax import lax
from jax.experimental import pallas as pl
from jax.experimental.pallas import tpu as pltpu
from jax.sharding import PartitionSpec as P

MESH = pl.DeviceIdType.MESH
F32 = jnp.float32
BF16 = jnp.bfloat16
CHUNKS = 8
LAGS = (1, 2, 4, 5, 6)
LANES = 128


def split(x):
    high = x.astype(BF16)
    return high, (x - high.astype(F32)).astype(BF16)


def mul(a, b):
    return lax.dot_general(a, b, (((1,), (0,)), ((), ())), preferred_element_type=F32)


def mul_t(a, b):
    return lax.dot_general(a, b, (((1,), (1,)), ((), ())), preferred_element_type=F32)


def kernel(shape, gsize, field, b2_ref, b3_ref, proj, gram, *scratch):
    (fbuf, w2f, w2, k3, k3f, core, rgz, pa, pb, ra, rb, sa, sb, xbuf, qo, qn, qf,
     tbuf, tin, obuf, gp, rg, fin,
     fsem, zs, zr, ys, yr, os_, or_, ns, nr_, fs, fr, g1s, g2s, ts, tr, gs, gr, hs, hr) = scratch
    nv, rows, depth, width = shape
    GX, GY, GZ = gsize
    rank = b2_ref.shape[0]
    tdim = b3_ref.shape[1]
    step = rows // CHUNKS
    pairs = step // 2
    sloc = rank // GZ
    cols = sloc * tdim
    nr = GY * GZ
    slab = rows // nr
    gx, gy, gz = lax.axis_index("gx"), lax.axis_index("gy"), lax.axis_index("gz")
    me = gy * GZ + gz

    def layer(d):
        other = lax.rem(me + d, nr)
        return other, (gx, other // GZ, lax.rem(other, GZ))

    def rows_of(k):
        return pl.ds(pl.multiple_of(k * step, step), step)

    def load(k):
        r = rows_of(k)
        return pltpu.make_async_copy(field.at[:, r], fbuf.at[:, r], fsem.at[k])

    for k in range(CHUNKS):
        load(k).start()

    barrier = pltpu.get_barrier_semaphore()
    for d in range(1, nr):
        pl.semaphore_signal(barrier, inc=1, device_id=layer(d)[1], device_id_type=MESH)
    for d in range(1, GX):
        pl.semaphore_signal(
            barrier, inc=1, device_id=(lax.rem(gx + d, GX), gy, gz), device_id_type=MESH
        )

    turned = b2_ref[...].T
    w2f[...] = jnp.zeros_like(w2f)
    for z in range(GZ):
        for v in range(nv):
            at = (z * nv + v) * sloc
            w2f[v * width : (v + 1) * width, at : at + sloc] = turned[
                :, z * sloc : (z + 1) * sloc
            ]
    high, low = split(w2f[...])
    w2[0] = high
    w2[1] = low
    k3f[...] = jnp.zeros_like(k3f)
    turned = b3_ref[...].T
    for i in range(4):
        k3f[i * tdim : (i + 1) * tdim, i * depth : (i + 1) * depth] = turned
    high, low = split(k3f[...])
    k3[0 : 4 * tdim] = high
    k3[4 * tdim :] = low

    def contract(k):
        parts = [
            split(fbuf[v, rows_of(k)].reshape(step * depth, width))
            for v in range(nv)
        ]
        high = jnp.concatenate([h for h, _ in parts], axis=1)
        low = jnp.concatenate([l for _, l in parts], axis=1)
        first = mul(high, w2[0]) + (mul(high, w2[1]) + mul(low, w2[0]))
        high, low = split(first)
        for j in range(pairs // 2):
            order = (2 * j, 2 * j + pairs, 2 * j + 1, 2 * j + 1 + pairs)
            h = jnp.concatenate([high[a * depth : (a + 1) * depth] for a in order], axis=0)
            l = jnp.concatenate([low[a * depth : (a + 1) * depth] for a in order], axis=0)
            one = mul(k3[...], h)
            two = mul(k3[0 : 4 * tdim], l)
            c = one[0 : 4 * tdim] + (one[4 * tdim :] + two)
            for z in range(GZ):
                core[k, z, j * 4 * tdim : (j + 1) * 4 * tdim] = c[
                    :, z * nv * sloc : (z + 1) * nv * sloc
                ]

    def gz_copies(k):
        out = []
        for d in range(1, GZ):
            peer = lax.rem(gz + d, GZ)
            out.append(
                pltpu.make_async_remote_copy(
                    src_ref=core.at[k, peer], dst_ref=rgz.at[k, d - 1],
                    send_sem=zs.at[k, d - 1], recv_sem=zr.at[k, d - 1],
                    device_id=(gx, gy, peer), device_id_type=MESH,
                )
            )
        return out

    def remote(src, dst, send, recv, where):
        return pltpu.make_async_remote_copy(
            src_ref=src, dst_ref=dst, send_sem=send, recv_sem=recv,
            device_id=where, device_id_type=MESH,
        )

    y, x = gy // 2, lax.rem(gy, 2)
    along_x = (gx, y * 2 + 1 - x, gz)
    along_y = (gx, (1 - y) * 2 + x, gz)

    def first_copies(k):
        return [
            remote(pa.at[k, 1 - x], ra.at[k], ys.at[k, 0], yr.at[k, 0], along_x),
            remote(pb.at[k, 1 - y], rb.at[k], ys.at[k, 1], yr.at[k, 1], along_y),
        ]

    def second_copies(k):
        return [
            remote(pa.at[k, x, 1 - y], sa.at[k], ys.at[k, 2], yr.at[k, 2], along_y),
            remote(pb.at[k, y, 1 - x], sb.at[k], ys.at[k, 3], yr.at[k, 3], along_x),
        ]

    side = gx // 2
    inner = (gx == 1) | (gx == 2)
    outer = jnp.logical_not(inner)
    mate = gx + 1 - 2 * lax.rem(gx, 2)
    far_inner, far_outer = 2 - side, 3 * (1 - side)
    hcols = cols // 2
    to_mate, over = (mate, gy, gz), (GX - 1 - gx, gy, gz)
    out_cols = pl.ds(pl.multiple_of(side * hcols, LANES), hcols)
    in_cols = pl.ds(pl.multiple_of((1 - side) * hcols, LANES), hcols)

    def whole_copy(k):
        r = rows_of(k)
        return remote(proj.at[r], qo.at[r], os_.at[k], or_.at[k], to_mate)

    def near_copy(k):
        r = rows_of(k)
        return remote(proj.at[r, out_cols], qn.at[r], ns.at[k], nr_.at[k], over)

    def far_copy(k):
        r = rows_of(k)
        return remote(qo.at[r, out_cols], qf.at[r], fs.at[k], fr.at[k], over)

    def near_on(k):
        r = rows_of(k)
        return remote(qn.at[r], qn.at[r], g1s.at[k], nr_.at[k], to_mate)

    def far_on(k):
        r = rows_of(k)
        return remote(qf.at[r], qf.at[r], g2s.at[k], fr.at[k], to_mate)

    def stage_a(k):
        load(k).wait()
        contract(k)

        @pl.when(k == 0)
        def _():
            pl.semaphore_wait(barrier, nr - 1 + GX - 1)

        for c in gz_copies(k):
            c.start()

    def stage_b(k):
        for c in gz_copies(k):
            c.wait_recv()
        total = core[k, gz]
        for d in range(GZ - 1):
            total = total + rgz[k, d]
        for q in range(pairs):
            t = total[q * LANES : (q + 1) * LANES].T
            for v in range(nv):
                piece = t[v * sloc : (v + 1) * sloc]
                if q < pairs // 2:
                    pa[k, v % 2, v // 2, q] = piece
                else:
                    pb[k, v // 2, v % 2, q - pairs // 2] = piece
        for c in first_copies(k):
            c.start()

    def stage_c(k):
        for c in first_copies(k):
            c.wait_recv()
        pa[k, x] = pa[k, x] + ra[k]
        pb[k, y] = pb[k, y] + rb[k]
        for c in second_copies(k):
            c.start()

    def stage_d(k):
        for c in second_copies(k):
            c.wait_recv()
        total = jnp.concatenate([pa[k, x, y] + sa[k], pb[k, y, x] + sb[k]], axis=0)
        xbuf[...] = total.reshape(pairs * sloc, LANES)
        lane = lax.broadcasted_iota(jnp.int32, (pairs, LANES), 1)
        first = lane < tdim
        done = []
        for p in range(sloc // 2):
            a = xbuf[pl.ds(2 * p, pairs, stride=sloc), :]
            b = xbuf[pl.ds(2 * p + 1, pairs, stride=sloc), :]
            done.append(
                jnp.concatenate(
                    [
                        jnp.where(first, a, pltpu.roll(b, tdim, 1)),
                        jnp.where(first, pltpu.roll(a, tdim, 1), b),
                    ],
                    axis=0,
                )
            )
        proj[rows_of(k), :] = jnp.concatenate(done, axis=1)

        @pl.when(outer)
        def _():
            whole_copy(k).start()

        @pl.when(inner)
        def _():
            near_copy(k).start()

    def stage_e(k):
        @pl.when(inner)
        def _():
            whole_copy(k).wait_recv()
            far_copy(k).start()
            near_copy(k).wait_recv()
            near_on(k).start()

    def stage_f(k):
        @pl.when(inner)
        def _():
            far_copy(k).wait_recv()
            far_on(k).start()

    stages = [stage_a, stage_b, stage_c, stage_d, stage_e, stage_f]

    @pl.loop(0, CHUNKS + LAGS[-1])
    def _(k):
        for stage, lag in zip(stages, (0,) + LAGS):
            pl.when((k >= lag) & (k < CHUNKS + lag))(functools.partial(stage, k - lag))

    ph, pw = split(proj[...])
    hh, hw = split(proj[:, in_cols])
    diag = mul_t(ph, ph) + (mul_t(ph, pw) + mul_t(pw, ph))

    @pl.when(outer)
    def _():
        @pl.loop(0, CHUNKS)
        def _(k):
            near_on(k).wait_recv()
            far_on(k).wait_recv()

    def pair(ah, aw, bh, bw):
        return mul_t(ah, bh) + (mul_t(ah, bw) + mul_t(aw, bh))

    bh, bw = split(qn[...])
    near = pair(hh, hw, bh, bw)
    tbuf[0] = pair(bh, bw, hh, hw)
    bh, bw = split(qf[...])
    far = pair(hh, hw, bh, bw)
    tbuf[1] = pair(bh, bw, hh, hw)
    kind = 1 - inner.astype(jnp.int32)
    swaps = [
        remote(tbuf.at[0], tin.at[kind], ts.at[0], tr.at[kind], (far_inner, gy, gz)),
        remote(tbuf.at[1], tin.at[kind], ts.at[1], tr.at[kind], (far_outer, gy, gz)),
    ]
    back = remote(tbuf.at[2], obuf, ts.at[2], tr.at[2], to_mate)
    for c in swaps:
        c.start()

    @pl.when(inner)
    def _():
        oh, ow = split(qo[...])
        tbuf[2] = pair(oh, ow, ph, pw)
        back.start()
        obuf[...] = pair(ph, pw, oh, ow)

    @pl.when(outer)
    def _():
        back.wait_recv()

    for i in range(2):
        remote(tbuf.at[i], tin.at[i], ts.at[i], tr.at[i], to_mate).wait_recv()
    near = near + tin[0]
    far = far + tin[1]
    beside = obuf[...]
    blocks = []
    for j in range(GX):
        blocks.append(
            jnp.where(
                gx == j, diag,
                jnp.where(mate == j, beside, jnp.where(far_inner == j, near, far)),
            )
        )
    whole = jnp.concatenate(blocks, axis=1) * F32(1.0 / (nv * rank * tdim))
    for r in range(nr):
        gp[r] = whole[r * slab : (r + 1) * slab]
    gather = []
    for d in range(1, nr):
        other, where = layer(d)
        gather.append(
            pltpu.make_async_remote_copy(
                src_ref=gp.at[other], dst_ref=rg.at[d - 1],
                send_sem=gs.at[d - 1], recv_sem=gr.at[d - 1],
                device_id=where, device_id_type=MESH,
            )
        )
    for c in gather:
        c.start()
    for c in gather:
        c.wait_recv()
    total = gp[me]
    for d in range(nr - 1):
        total = total + rg[d]
    fin[me] = total
    spread = []
    for d in range(1, nr):
        other, where = layer(d)
        spread.append(
            pltpu.make_async_remote_copy(
                src_ref=fin.at[me], dst_ref=fin.at[me],
                send_sem=hs.at[d - 1], recv_sem=hr.at[d - 1],
                device_id=where, device_id_type=MESH,
            )
        )
    for c in spread:
        c.start()
    for c in spread:
        c.wait_recv()
    for r in range(nr):
        gram[r * slab : (r + 1) * slab, :] = fin[r]
    for c in swaps + gather + spread:
        c.wait_send()

    @pl.when(inner)
    def _():
        back.wait_send()

    @pl.loop(0, CHUNKS)
    def _(k):
        for c in gz_copies(k) + first_copies(k) + second_copies(k):
            c.wait_send()

        @pl.when(outer)
        def _():
            whole_copy(k).wait_send()

        @pl.when(inner)
        def _():
            for c in (near_copy(k), far_copy(k), near_on(k), far_on(k)):
                c.wait_send()


def body(gsize, field, basis_two, basis_three):
    nv, rows, depth, width = field.shape
    rank, tdim = basis_two.shape[1], basis_three.shape[1]
    GX, GY, GZ = gsize
    assert GX == 4 and GY == 4 and nv == 4 and 4 * depth == 256 and 2 * tdim == LANES
    sloc = rank // GZ
    cols = sloc * tdim
    step = rows // CHUNKS
    pairs = step // 2
    nr = GY * GZ
    slab = rows // nr
    dma = pltpu.SemaphoreType.DMA
    vmem = pl.BlockSpec(memory_space=pltpu.VMEM)
    return pl.pallas_call(
        functools.partial(kernel, field.shape, gsize),
        out_shape=(
            jax.ShapeDtypeStruct((rows, cols), F32),
            jax.ShapeDtypeStruct((rows, GX * rows), F32),
        ),
        in_specs=[pl.BlockSpec(memory_space=pl.ANY), vmem, vmem],
        out_specs=(vmem, vmem),
        scratch_shapes=[
            pltpu.VMEM(field.shape, F32),
            pltpu.VMEM((nv * width, nv * rank), F32),
            pltpu.VMEM((2, nv * width, nv * rank), BF16),
            pltpu.VMEM((8 * tdim, 4 * depth), BF16),
            pltpu.VMEM((4 * tdim, 4 * depth), F32),
            pltpu.VMEM((CHUNKS, GZ, step * tdim, nv * sloc), F32),
            pltpu.VMEM((CHUNKS, GZ - 1, step * tdim, nv * sloc), F32),
            pltpu.VMEM((CHUNKS, 2, 2, pairs // 2, sloc, LANES), F32),
            pltpu.VMEM((CHUNKS, 2, 2, pairs // 2, sloc, LANES), F32),
            pltpu.VMEM((CHUNKS, 2, pairs // 2, sloc, LANES), F32),
            pltpu.VMEM((CHUNKS, 2, pairs // 2, sloc, LANES), F32),
            pltpu.VMEM((CHUNKS, pairs // 2, sloc, LANES), F32),
            pltpu.VMEM((CHUNKS, pairs // 2, sloc, LANES), F32),
            pltpu.VMEM((pairs * sloc, LANES), F32),
            pltpu.VMEM((rows, cols), F32),
            pltpu.VMEM((rows, cols // 2), F32),
            pltpu.VMEM((rows, cols // 2), F32),
            pltpu.VMEM((3, rows, rows), F32),
            pltpu.VMEM((2, rows, rows), F32),
            pltpu.VMEM((rows, rows), F32),
            pltpu.VMEM((nr, slab, GX * rows), F32),
            pltpu.VMEM((nr - 1, slab, GX * rows), F32),
            pltpu.VMEM((nr, slab, GX * rows), F32),
            dma((CHUNKS,)),
            dma((CHUNKS, GZ - 1)),
            dma((CHUNKS, GZ - 1)),
            dma((CHUNKS, 4)),
            dma((CHUNKS, 4)),
            dma((CHUNKS,)),
            dma((CHUNKS,)),
            dma((CHUNKS,)),
            dma((CHUNKS,)),
            dma((CHUNKS,)),
            dma((CHUNKS,)),
            dma((CHUNKS,)),
            dma((CHUNKS,)),
            dma((3,)),
            dma((3,)),
            dma((nr - 1,)),
            dma((nr - 1,)),
            dma((nr - 1,)),
            dma((nr - 1,)),
        ],
        compiler_params=pltpu.CompilerParams(
            collective_id=0, has_side_effects=True, vmem_limit_bytes=56 * 2**20
        ),
    )(field, basis_two.T, basis_three)


def solution(mesh):
    placed = (P(None, "gx", "gz", "gy"), P("gy", None), P("gz", None))
    gsize = tuple(mesh.shape[name] for name in ("gx", "gy", "gz"))
    return jax.shard_map(
        functools.partial(body, gsize),
        mesh=mesh,
        in_specs=placed,
        out_specs=(P("gx", ("gy", "gz")), P("gx", None)),
        check_vma=False,
    )
```

```python
import functools

import jax
import jax.numpy as jnp
from jax import lax
from jax.experimental import pallas as pl
from jax.experimental.pallas import tpu as pltpu
from jax.sharding import PartitionSpec as P

MESH = pl.DeviceIdType.MESH
F32 = jnp.float32
BF16 = jnp.bfloat16
CHUNKS = 8
LAG_B = 2
LAG = 6
LANES = 128


def split(x):
    high = x.astype(BF16)
    return high, (x - high.astype(F32)).astype(BF16)


def mul(a, b):
    return lax.dot_general(a, b, (((1,), (0,)), ((), ())), preferred_element_type=F32)


def mul_t(a, b):
    return lax.dot_general(a, b, (((1,), (1,)), ((), ())), preferred_element_type=F32)


def kernel(shape, gsize, field, b2_ref, b3_ref, proj, gram, *scratch):
    (fbuf, w2f, w2, k3, k3f, core, rgz, half, rgy, xbuf, q1, q2, tbuf, t1, t2, gp, rg, fin,
     fsem, zs, zr, ys, yr, as_, ar, bs, br, ts, tr, gs, gr, hs, hr) = scratch
    nv, rows, depth, width = shape
    GX, GY, GZ = gsize
    rank = b2_ref.shape[0]
    tdim = b3_ref.shape[1]
    step = rows // CHUNKS
    pairs = step // 2
    sloc = rank // GZ
    cols = sloc * tdim
    nr = GY * GZ
    slab = rows // nr
    gx, gy, gz = lax.axis_index("gx"), lax.axis_index("gy"), lax.axis_index("gz")
    me = gy * GZ + gz

    def layer(d):
        other = lax.rem(me + d, nr)
        return other, (gx, other // GZ, lax.rem(other, GZ))

    def rows_of(k):
        return pl.ds(pl.multiple_of(k * step, step), step)

    def load(k):
        r = rows_of(k)
        return pltpu.make_async_copy(field.at[:, r], fbuf.at[:, r], fsem.at[k])

    for k in range(CHUNKS):
        load(k).start()

    barrier = pltpu.get_barrier_semaphore()
    for d in range(1, nr):
        pl.semaphore_signal(barrier, inc=1, device_id=layer(d)[1], device_id_type=MESH)
    for d in range(1, GX):
        pl.semaphore_signal(
            barrier, inc=1, device_id=(lax.rem(gx + d, GX), gy, gz), device_id_type=MESH
        )

    turned = b2_ref[...].T
    w2f[...] = jnp.zeros_like(w2f)
    for z in range(GZ):
        for v in range(nv):
            at = (z * nv + v) * sloc
            w2f[v * width : (v + 1) * width, at : at + sloc] = turned[
                :, z * sloc : (z + 1) * sloc
            ]
    high, low = split(w2f[...])
    w2[0] = high
    w2[1] = low
    k3f[...] = jnp.zeros_like(k3f)
    turned = b3_ref[...].T
    for i in range(4):
        k3f[i * tdim : (i + 1) * tdim, i * depth : (i + 1) * depth] = turned
    high, low = split(k3f[...])
    k3[0 : 4 * tdim] = high
    k3[4 * tdim :] = low

    def contract(k):
        parts = [
            split(fbuf[v, rows_of(k)].reshape(step * depth, width))
            for v in range(nv)
        ]
        high = jnp.concatenate([h for h, _ in parts], axis=1)
        low = jnp.concatenate([l for _, l in parts], axis=1)
        first = mul(high, w2[0]) + (mul(high, w2[1]) + mul(low, w2[0]))
        high, low = split(first)
        for j in range(pairs // 2):
            order = (2 * j, 2 * j + pairs, 2 * j + 1, 2 * j + 1 + pairs)
            h = jnp.concatenate([high[a * depth : (a + 1) * depth] for a in order], axis=0)
            l = jnp.concatenate([low[a * depth : (a + 1) * depth] for a in order], axis=0)
            one = mul(k3[...], h)
            two = mul(k3[0 : 4 * tdim], l)
            c = one[0 : 4 * tdim] + (one[4 * tdim :] + two)
            for z in range(GZ):
                core[k, z, j * 4 * tdim : (j + 1) * 4 * tdim] = c[
                    :, z * nv * sloc : (z + 1) * nv * sloc
                ]

    def gz_copies(k):
        out = []
        for d in range(1, GZ):
            peer = lax.rem(gz + d, GZ)
            out.append(
                pltpu.make_async_remote_copy(
                    src_ref=core.at[k, peer], dst_ref=rgz.at[k, d - 1],
                    send_sem=zs.at[k, d - 1], recv_sem=zr.at[k, d - 1],
                    device_id=(gx, gy, peer), device_id_type=MESH,
                )
            )
        return out

    def gy_copies(k):
        out = []
        for d in range(1, GY):
            peer = lax.rem(gy + d, GY)
            out.append(
                pltpu.make_async_remote_copy(
                    src_ref=half.at[k, peer], dst_ref=rgy.at[k, d - 1],
                    send_sem=ys.at[k, d - 1], recv_sem=yr.at[k, d - 1],
                    device_id=(gx, peer, gz), device_id_type=MESH,
                )
            )
        return out

    upper = lax.rem(gx + 1, GX)
    across = lax.rem(gx + 2, GX)
    hcols = cols // 2
    sent = pl.multiple_of((across // 2) * hcols, LANES)
    mine = pl.multiple_of((gx // 2) * hcols, LANES)

    def gx_copies(k):
        r = rows_of(k)
        return [
            pltpu.make_async_remote_copy(
                src_ref=proj.at[r], dst_ref=q1.at[r],
                send_sem=as_.at[k], recv_sem=ar.at[k],
                device_id=(upper, gy, gz), device_id_type=MESH,
            ),
            pltpu.make_async_remote_copy(
                src_ref=proj.at[r, pl.ds(sent, hcols)], dst_ref=q2.at[r],
                send_sem=bs.at[k], recv_sem=br.at[k],
                device_id=(across, gy, gz), device_id_type=MESH,
            ),
        ]

    def stage_a(k):
        load(k).wait()
        contract(k)

        @pl.when(k == 0)
        def _():
            pl.semaphore_wait(barrier, nr - 1 + GX - 1)

        for c in gz_copies(k):
            c.start()

    def stage_b(k):
        for c in gz_copies(k):
            c.wait_recv()
        total = core[k, gz]
        for d in range(GZ - 1):
            total = total + rgz[k, d]
        for q in range(pairs):
            t = total[q * LANES : (q + 1) * LANES].T
            for v in range(nv):
                half[k, v, q] = t[v * sloc : (v + 1) * sloc]
        for c in gy_copies(k):
            c.start()

    def stage_c(k):
        for c in gy_copies(k):
            c.wait_recv()
        total = half[k, gy]
        for d in range(GY - 1):
            total = total + rgy[k, d]
        xbuf[...] = total.reshape(pairs * sloc, LANES)
        lane = lax.broadcasted_iota(jnp.int32, (pairs, LANES), 1)
        first = lane < tdim
        done = []
        for p in range(sloc // 2):
            a = xbuf[pl.ds(2 * p, pairs, stride=sloc), :]
            b = xbuf[pl.ds(2 * p + 1, pairs, stride=sloc), :]
            done.append(
                jnp.concatenate(
                    [
                        jnp.where(first, a, pltpu.roll(b, tdim, 1)),
                        jnp.where(first, pltpu.roll(a, tdim, 1), b),
                    ],
                    axis=0,
                )
            )
        proj[rows_of(k), :] = jnp.concatenate(done, axis=1)
        for c in gx_copies(k):
            c.start()

    @pl.loop(0, CHUNKS + LAG)
    def _(k):
        @pl.when(k < CHUNKS)
        def _():
            stage_a(k)

        @pl.when((k >= LAG_B) & (k < CHUNKS + LAG_B))
        def _():
            stage_b(k - LAG_B)

        @pl.when(k >= LAG)
        def _():
            stage_c(k - LAG)

    def pair(both, high, other):
        h, l = split(other)
        one = mul_t(both, h)
        return one[0:rows] + (one[rows:] + mul_t(high, l))

    ph, pw = split(proj[...])
    hh, hw = split(proj[:, pl.ds(mine, hcols)])
    both = jnp.concatenate([ph, pw], axis=0)
    half_both = jnp.concatenate([hh, hw], axis=0)
    diag = pair(both, ph, proj[...])

    @pl.loop(0, CHUNKS)
    def _(k):
        for c in gx_copies(k):
            c.wait_recv()

    n1 = pair(both, ph, q1[...])
    n2 = pair(half_both, hh, q2[...])
    tbuf[...] = jnp.concatenate([n1.T, n2.T], axis=1)
    lower = lax.rem(gx + GX - 1, GX)
    swaps = [
        pltpu.make_async_remote_copy(
            src_ref=tbuf, dst_ref=t1, send_sem=ts.at[0], recv_sem=tr.at[0],
            device_id=(lower, gy, gz), device_id_type=MESH,
        ),
        pltpu.make_async_remote_copy(
            src_ref=tbuf, dst_ref=t2, send_sem=ts.at[1], recv_sem=tr.at[1],
            device_id=(across, gy, gz), device_id_type=MESH,
        ),
    ]
    for c in swaps:
        c.start()
    for c in swaps:
        c.wait_recv()
    r1 = t1[:, 0:rows]
    n2 = n2 + t2[:, rows:]
    blocks = []
    for j in range(GX):
        d = lax.rem(j - gx + GX, GX)
        blocks.append(
            jnp.where(d == 0, diag, jnp.where(d == 1, r1, jnp.where(d == 2, n2, n1)))
        )
    whole = jnp.concatenate(blocks, axis=1) * F32(1.0 / (nv * rank * tdim))
    for r in range(nr):
        gp[r] = whole[r * slab : (r + 1) * slab]
    gather = []
    for d in range(1, nr):
        other, where = layer(d)
        gather.append(
            pltpu.make_async_remote_copy(
                src_ref=gp.at[other], dst_ref=rg.at[d - 1],
                send_sem=gs.at[d - 1], recv_sem=gr.at[d - 1],
                device_id=where, device_id_type=MESH,
            )
        )
    for c in gather:
        c.start()
    for c in gather:
        c.wait_recv()
    total = gp[me]
    for d in range(nr - 1):
        total = total + rg[d]
    fin[me] = total
    spread = []
    for d in range(1, nr):
        other, where = layer(d)
        spread.append(
            pltpu.make_async_remote_copy(
                src_ref=fin.at[me], dst_ref=fin.at[me],
                send_sem=hs.at[d - 1], recv_sem=hr.at[d - 1],
                device_id=where, device_id_type=MESH,
            )
        )
    for c in spread:
        c.start()
    for c in spread:
        c.wait_recv()
    for r in range(nr):
        gram[r * slab : (r + 1) * slab, :] = fin[r]
    for c in swaps + gather + spread:
        c.wait_send()

    @pl.loop(0, CHUNKS)
    def _(k):
        for c in gz_copies(k) + gy_copies(k) + gx_copies(k):
            c.wait_send()


def settle(proj_in, gram_in, proj, gram, sem):
    copies = [
        pltpu.make_async_copy(proj_in, proj, sem.at[0]),
        pltpu.make_async_copy(gram_in, gram, sem.at[1]),
    ]
    for c in copies:
        c.start()
    for c in copies:
        c.wait()


def body(gsize, field, basis_two, basis_three):
    nv, rows, depth, width = field.shape
    rank, tdim = basis_two.shape[1], basis_three.shape[1]
    GX, GY, GZ = gsize
    assert GX == 4 and GY == nv and 4 * depth == 256 and 2 * tdim == LANES
    sloc = rank // GZ
    cols = sloc * tdim
    step = rows // CHUNKS
    pairs = step // 2
    nr = GY * GZ
    slab = rows // nr
    dma = pltpu.SemaphoreType.DMA
    vmem = pl.BlockSpec(memory_space=pltpu.VMEM)
    results = pl.pallas_call(
        functools.partial(kernel, field.shape, gsize),
        out_shape=(
            jax.ShapeDtypeStruct((rows, cols), F32),
            jax.ShapeDtypeStruct((rows, GX * rows), F32),
        ),
        in_specs=[pl.BlockSpec(memory_space=pl.ANY), vmem, vmem],
        out_specs=(vmem, vmem),
        scratch_shapes=[
            pltpu.VMEM(field.shape, F32),
            pltpu.VMEM((nv * width, nv * rank), F32),
            pltpu.VMEM((2, nv * width, nv * rank), BF16),
            pltpu.VMEM((8 * tdim, 4 * depth), BF16),
            pltpu.VMEM((4 * tdim, 4 * depth), F32),
            pltpu.VMEM((CHUNKS, GZ, step * tdim, nv * sloc), F32),
            pltpu.VMEM((CHUNKS, GZ - 1, step * tdim, nv * sloc), F32),
            pltpu.VMEM((CHUNKS, nv, pairs, sloc, LANES), F32),
            pltpu.VMEM((CHUNKS, GY - 1, pairs, sloc, LANES), F32),
            pltpu.VMEM((pairs * sloc, LANES), F32),
            pltpu.VMEM((rows, cols), F32),
            pltpu.VMEM((rows, cols // 2), F32),
            pltpu.VMEM((rows, 2 * rows), F32),
            pltpu.VMEM((rows, 2 * rows), F32),
            pltpu.VMEM((rows, 2 * rows), F32),
            pltpu.VMEM((nr, slab, GX * rows), F32),
            pltpu.VMEM((nr - 1, slab, GX * rows), F32),
            pltpu.VMEM((nr, slab, GX * rows), F32),
            dma((CHUNKS,)),
            dma((CHUNKS, GZ - 1)),
            dma((CHUNKS, GZ - 1)),
            dma((CHUNKS, GY - 1)),
            dma((CHUNKS, GY - 1)),
            dma((CHUNKS,)),
            dma((CHUNKS,)),
            dma((CHUNKS,)),
            dma((CHUNKS,)),
            dma((2,)),
            dma((2,)),
            dma((nr - 1,)),
            dma((nr - 1,)),
            dma((nr - 1,)),
            dma((nr - 1,)),
        ],
        compiler_params=pltpu.CompilerParams(
            collective_id=0, has_side_effects=True, vmem_limit_bytes=56 * 2**20
        ),
    )(field, basis_two.T, basis_three)
    anywhere = pl.BlockSpec(memory_space=pl.ANY)
    return pl.pallas_call(
        settle,
        out_shape=tuple(jax.ShapeDtypeStruct(r.shape, r.dtype) for r in results),
        in_specs=[anywhere, anywhere],
        out_specs=(anywhere, anywhere),
        scratch_shapes=[dma((2,))],
    )(*results)


def solution(mesh):
    placed = (P(None, "gx", "gz", "gy"), P("gy", None), P("gz", None))
    gsize = tuple(mesh.shape[name] for name in ("gx", "gy", "gz"))
    return jax.shard_map(
        functools.partial(body, gsize),
        mesh=mesh,
        in_specs=placed,
        out_specs=(P("gx", ("gy", "gz")), P("gx", None)),
        check_vma=False,
    )
```

```python
import functools

import jax
import jax.numpy as jnp
from jax import lax
from jax.experimental import pallas as pl
from jax.experimental.pallas import tpu as pltpu
from jax.sharding import PartitionSpec as P

MESH = pl.DeviceIdType.MESH
F32 = jnp.float32
BF16 = jnp.bfloat16
CHUNKS = 8
LAG_B = 1
LAG = 2
LANES = 128


def split(x):
    high = x.astype(BF16)
    return high, (x - high.astype(F32)).astype(BF16)


def mul(a, b):
    return lax.dot_general(a, b, (((1,), (0,)), ((), ())), preferred_element_type=F32)


def mul_t(a, b):
    return lax.dot_general(a, b, (((1,), (1,)), ((), ())), preferred_element_type=F32)


def kernel(shape, gsize, field, b2_ref, b3_ref, proj, gram, *scratch):
    (fbuf, w2f, w2, k3, k3f, core, rgz, half, rgy, xbuf, q1, q2, tbuf, t1, t2, gp, rg, fin,
     fsem, zs, zr, ys, yr, as_, ar, bs, br, ts, tr, gs, gr, hs, hr) = scratch
    nv, rows, depth, width = shape
    GX, GY, GZ = gsize
    rank = b2_ref.shape[0]
    tdim = b3_ref.shape[1]
    step = rows // CHUNKS
    pairs = step // 2
    sloc = rank // GZ
    cols = sloc * tdim
    nr = GY * GZ
    slab = rows // nr
    gx, gy, gz = lax.axis_index("gx"), lax.axis_index("gy"), lax.axis_index("gz")
    me = gy * GZ + gz

    def layer(d):
        other = lax.rem(me + d, nr)
        return other, (gx, other // GZ, lax.rem(other, GZ))

    def rows_of(k):
        return pl.ds(pl.multiple_of(k * step, step), step)

    def load(k, v):
        r = rows_of(k)
        return pltpu.make_async_copy(field.at[v, r], fbuf.at[v, r], fsem.at[k, v])

    for k in range(CHUNKS):
        for v in range(nv):
            load(k, v).start()

    barrier = pltpu.get_barrier_semaphore()
    for d in range(1, nr):
        pl.semaphore_signal(barrier, inc=1, device_id=layer(d)[1], device_id_type=MESH)
    for d in range(1, GX):
        pl.semaphore_signal(
            barrier, inc=1, device_id=(lax.rem(gx + d, GX), gy, gz), device_id_type=MESH
        )

    turned = b2_ref[...].T
    w2f[...] = jnp.zeros_like(w2f)
    for z in range(GZ):
        for v in range(nv):
            at = (z * nv + v) * sloc
            w2f[v * width : (v + 1) * width, at : at + sloc] = turned[
                :, z * sloc : (z + 1) * sloc
            ]
    high, low = split(w2f[...])
    w2[0] = high
    w2[1] = low
    k3f[...] = jnp.zeros_like(k3f)
    turned = b3_ref[...].T
    for i in range(4):
        k3f[i * tdim : (i + 1) * tdim, i * depth : (i + 1) * depth] = turned
    high, low = split(k3f[...])
    k3[0 : 4 * tdim] = high
    k3[4 * tdim :] = low

    def contract(k):
        parts = [
            split(fbuf[v, rows_of(k)].reshape(step * depth, width))
            for v in range(nv)
        ]
        high = jnp.concatenate([h for h, _ in parts], axis=1)
        low = jnp.concatenate([l for _, l in parts], axis=1)
        first = mul(high, w2[0]) + (mul(high, w2[1]) + mul(low, w2[0]))
        high, low = split(first)
        for j in range(pairs // 2):
            order = (2 * j, 2 * j + pairs, 2 * j + 1, 2 * j + 1 + pairs)
            h = jnp.concatenate([high[a * depth : (a + 1) * depth] for a in order], axis=0)
            l = jnp.concatenate([low[a * depth : (a + 1) * depth] for a in order], axis=0)
            one = mul(k3[...], h)
            two = mul(k3[0 : 4 * tdim], l)
            c = one[0 : 4 * tdim] + (one[4 * tdim :] + two)
            for z in range(GZ):
                core[k, z, j * 4 * tdim : (j + 1) * 4 * tdim] = c[
                    :, z * nv * sloc : (z + 1) * nv * sloc
                ]

    def gz_copies(k):
        out = []
        for d in range(1, GZ):
            peer = lax.rem(gz + d, GZ)
            out.append(
                pltpu.make_async_remote_copy(
                    src_ref=core.at[k, peer], dst_ref=rgz.at[k, d - 1],
                    send_sem=zs.at[k, d - 1], recv_sem=zr.at[k, d - 1],
                    device_id=(gx, gy, peer), device_id_type=MESH,
                )
            )
        return out

    def gy_copies(k):
        out = []
        for d in range(1, GY):
            peer = lax.rem(gy + d, GY)
            out.append(
                pltpu.make_async_remote_copy(
                    src_ref=half.at[k, peer], dst_ref=rgy.at[k, d - 1],
                    send_sem=ys.at[k, d - 1], recv_sem=yr.at[k, d - 1],
                    device_id=(gx, peer, gz), device_id_type=MESH,
                )
            )
        return out

    upper = lax.rem(gx + 1, GX)
    across = lax.rem(gx + 2, GX)
    hcols = cols // 2
    sent = pl.multiple_of((across // 2) * hcols, LANES)
    mine = pl.multiple_of((gx // 2) * hcols, LANES)

    def gx_copies(k):
        r = rows_of(k)
        return [
            pltpu.make_async_remote_copy(
                src_ref=proj.at[r], dst_ref=q1.at[r],
                send_sem=as_.at[k], recv_sem=ar.at[k],
                device_id=(upper, gy, gz), device_id_type=MESH,
            ),
            pltpu.make_async_remote_copy(
                src_ref=proj.at[r, pl.ds(sent, hcols)], dst_ref=q2.at[r],
                send_sem=bs.at[k], recv_sem=br.at[k],
                device_id=(across, gy, gz), device_id_type=MESH,
            ),
        ]

    def stage_a(k):
        for v in range(nv):
            load(k, v).wait()
        contract(k)

        @pl.when(k == 0)
        def _():
            pl.semaphore_wait(barrier, nr - 1 + GX - 1)

        for c in gz_copies(k):
            c.start()

    def stage_b(k):
        for c in gz_copies(k):
            c.wait_recv()
        total = core[k, gz]
        for d in range(GZ - 1):
            total = total + rgz[k, d]
        for q in range(pairs):
            t = total[q * LANES : (q + 1) * LANES].T
            for v in range(nv):
                half[k, v, q] = t[v * sloc : (v + 1) * sloc]
        for c in gy_copies(k):
            c.start()

    def stage_c(k):
        for c in gy_copies(k):
            c.wait_recv()
        total = half[k, gy]
        for d in range(GY - 1):
            total = total + rgy[k, d]
        xbuf[...] = total.reshape(pairs * sloc, LANES)
        lane = lax.broadcasted_iota(jnp.int32, (pairs, LANES), 1)
        first = lane < tdim
        done = []
        for p in range(sloc // 2):
            a = xbuf[pl.ds(2 * p, pairs, stride=sloc), :]
            b = xbuf[pl.ds(2 * p + 1, pairs, stride=sloc), :]
            done.append(
                jnp.concatenate(
                    [
                        jnp.where(first, a, pltpu.roll(b, tdim, 1)),
                        jnp.where(first, pltpu.roll(a, tdim, 1), b),
                    ],
                    axis=0,
                )
            )
        proj[rows_of(k), :] = jnp.concatenate(done, axis=1)
        for c in gx_copies(k):
            c.start()

    @pl.loop(0, CHUNKS + LAG)
    def _(k):
        @pl.when(k < CHUNKS)
        def _():
            stage_a(k)

        @pl.when((k >= LAG_B) & (k < CHUNKS + LAG_B))
        def _():
            stage_b(k - LAG_B)

        @pl.when(k >= LAG)
        def _():
            stage_c(k - LAG)

    def pair(both, high, other):
        h, l = split(other)
        one = mul_t(both, h)
        return one[0:rows] + (one[rows:] + mul_t(high, l))

    ph, pw = split(proj[...])
    hh, hw = split(proj[:, pl.ds(mine, hcols)])
    both = jnp.concatenate([ph, pw], axis=0)
    half_both = jnp.concatenate([hh, hw], axis=0)
    diag = pair(both, ph, proj[...])

    @pl.loop(0, CHUNKS)
    def _(k):
        for c in gx_copies(k):
            c.wait_recv()

    n1 = pair(both, ph, q1[...])
    n2 = pair(half_both, hh, q2[...])
    tbuf[...] = jnp.concatenate([n1.T, n2.T], axis=1)
    lower = lax.rem(gx + GX - 1, GX)
    swaps = [
        pltpu.make_async_remote_copy(
            src_ref=tbuf, dst_ref=t1, send_sem=ts.at[0], recv_sem=tr.at[0],
            device_id=(lower, gy, gz), device_id_type=MESH,
        ),
        pltpu.make_async_remote_copy(
            src_ref=tbuf, dst_ref=t2, send_sem=ts.at[1], recv_sem=tr.at[1],
            device_id=(across, gy, gz), device_id_type=MESH,
        ),
    ]
    for c in swaps:
        c.start()
    for c in swaps:
        c.wait_recv()
    r1 = t1[:, 0:rows]
    n2 = n2 + t2[:, rows:]
    blocks = []
    for j in range(GX):
        d = lax.rem(j - gx + GX, GX)
        blocks.append(
            jnp.where(d == 0, diag, jnp.where(d == 1, r1, jnp.where(d == 2, n2, n1)))
        )
    whole = jnp.concatenate(blocks, axis=1) * F32(1.0 / (nv * rank * tdim))
    for r in range(nr):
        gp[r] = whole[r * slab : (r + 1) * slab]
    gather = []
    for d in range(1, nr):
        other, where = layer(d)
        gather.append(
            pltpu.make_async_remote_copy(
                src_ref=gp.at[other], dst_ref=rg.at[d - 1],
                send_sem=gs.at[d - 1], recv_sem=gr.at[d - 1],
                device_id=where, device_id_type=MESH,
            )
        )
    for c in gather:
        c.start()
    for c in gather:
        c.wait_recv()
    total = gp[me]
    for d in range(nr - 1):
        total = total + rg[d]
    fin[me] = total
    spread = []
    for d in range(1, nr):
        other, where = layer(d)
        spread.append(
            pltpu.make_async_remote_copy(
                src_ref=fin.at[me], dst_ref=fin.at[me],
                send_sem=hs.at[d - 1], recv_sem=hr.at[d - 1],
                device_id=where, device_id_type=MESH,
            )
        )
    for c in spread:
        c.start()
    for c in spread:
        c.wait_recv()
    for r in range(nr):
        gram[r * slab : (r + 1) * slab, :] = fin[r]
    for c in swaps + gather + spread:
        c.wait_send()

    @pl.loop(0, CHUNKS)
    def _(k):
        for c in gz_copies(k) + gy_copies(k) + gx_copies(k):
            c.wait_send()


def body(gsize, field, basis_two, basis_three):
    nv, rows, depth, width = field.shape
    rank, tdim = basis_two.shape[1], basis_three.shape[1]
    GX, GY, GZ = gsize
    assert GX == 4 and GY == nv and 4 * depth == 256 and 2 * tdim == LANES
    sloc = rank // GZ
    cols = sloc * tdim
    step = rows // CHUNKS
    pairs = step // 2
    nr = GY * GZ
    slab = rows // nr
    dma = pltpu.SemaphoreType.DMA
    vmem = pl.BlockSpec(memory_space=pltpu.VMEM)
    return pl.pallas_call(
        functools.partial(kernel, field.shape, gsize),
        out_shape=(
            jax.ShapeDtypeStruct((rows, cols), F32),
            jax.ShapeDtypeStruct((rows, GX * rows), F32),
        ),
        in_specs=[pl.BlockSpec(memory_space=pl.ANY), vmem, vmem],
        out_specs=(vmem, vmem),
        scratch_shapes=[
            pltpu.VMEM(field.shape, F32),
            pltpu.VMEM((nv * width, nv * rank), F32),
            pltpu.VMEM((2, nv * width, nv * rank), BF16),
            pltpu.VMEM((8 * tdim, 4 * depth), BF16),
            pltpu.VMEM((4 * tdim, 4 * depth), F32),
            pltpu.VMEM((CHUNKS, GZ, step * tdim, nv * sloc), F32),
            pltpu.VMEM((CHUNKS, GZ - 1, step * tdim, nv * sloc), F32),
            pltpu.VMEM((CHUNKS, nv, pairs, sloc, LANES), F32),
            pltpu.VMEM((CHUNKS, GY - 1, pairs, sloc, LANES), F32),
            pltpu.VMEM((pairs * sloc, LANES), F32),
            pltpu.VMEM((rows, cols), F32),
            pltpu.VMEM((rows, cols // 2), F32),
            pltpu.VMEM((rows, 2 * rows), F32),
            pltpu.VMEM((rows, 2 * rows), F32),
            pltpu.VMEM((rows, 2 * rows), F32),
            pltpu.VMEM((nr, slab, GX * rows), F32),
            pltpu.VMEM((nr - 1, slab, GX * rows), F32),
            pltpu.VMEM((nr, slab, GX * rows), F32),
            dma((CHUNKS, nv)),
            dma((CHUNKS, GZ - 1)),
            dma((CHUNKS, GZ - 1)),
            dma((CHUNKS, GY - 1)),
            dma((CHUNKS, GY - 1)),
            dma((CHUNKS,)),
            dma((CHUNKS,)),
            dma((CHUNKS,)),
            dma((CHUNKS,)),
            dma((2,)),
            dma((2,)),
            dma((nr - 1,)),
            dma((nr - 1,)),
            dma((nr - 1,)),
            dma((nr - 1,)),
        ],
        compiler_params=pltpu.CompilerParams(
            collective_id=0, has_side_effects=True, vmem_limit_bytes=56 * 2**20
        ),
    )(field, basis_two.T, basis_three)


def solution(mesh):
    placed = (P(None, "gx", "gz", "gy"), P("gy", None), P("gz", None))
    gsize = tuple(mesh.shape[name] for name in ("gx", "gy", "gz"))
    return jax.shard_map(
        functools.partial(body, gsize),
        mesh=mesh,
        in_specs=placed,
        out_specs=(P("gx", ("gy", "gz")), P("gx", None)),
        check_vma=False,
    )
```

```python
import functools

import jax
import jax.numpy as jnp
from jax import lax
from jax.experimental import pallas as pl
from jax.experimental.pallas import tpu as pltpu
from jax.sharding import PartitionSpec as P

MESH = pl.DeviceIdType.MESH
F32 = jnp.float32
BF16 = jnp.bfloat16
CHUNKS = 8
LAG = 3
LANES = 128


def split(x):
    high = x.astype(BF16)
    return high, (x - high.astype(F32)).astype(BF16)


def mul(a, b):
    return lax.dot_general(a, b, (((1,), (0,)), ((), ())), preferred_element_type=F32)


def mul_t(a, b):
    return lax.dot_general(a, b, (((1,), (1,)), ((), ())), preferred_element_type=F32)


def kernel(shape, gsize, field, b2_ref, b3_ref, proj, gram, *scratch):
    (fbuf, w2, k3, k3f, core, rgz, half, rgy, xbuf, q1, q2, tbuf, t1, t2, gp, rg, fin,
     fsem, zs, zr, ys, yr, as_, ar, bs, br, ts, tr, gs, gr, hs, hr) = scratch
    nv, rows, depth, width = shape
    GX, GY, GZ = gsize
    rank = b2_ref.shape[0]
    tdim = b3_ref.shape[1]
    step = rows // CHUNKS
    pairs = step // 2
    sloc = rank // GZ
    cols = sloc * tdim
    nr = GY * GZ
    slab = rows // nr
    gx, gy, gz = lax.axis_index("gx"), lax.axis_index("gy"), lax.axis_index("gz")
    me = gy * GZ + gz

    def layer(d):
        other = lax.rem(me + d, nr)
        return other, (gx, other // GZ, lax.rem(other, GZ))

    loads = [
        pltpu.make_async_copy(
            field.at[:, pl.ds(k * step, step)], fbuf.at[:, pl.ds(k * step, step)], fsem.at[k]
        )
        for k in range(CHUNKS)
    ]
    for load in loads:
        load.start()

    barrier = pltpu.get_barrier_semaphore()
    for d in range(1, nr):
        pl.semaphore_signal(barrier, inc=1, device_id=layer(d)[1], device_id_type=MESH)
    for d in range(1, GX):
        pl.semaphore_signal(
            barrier, inc=1, device_id=(lax.rem(gx + d, GX), gy, gz), device_id_type=MESH
        )

    high, low = split(b2_ref[...])
    w2[0:rank, :] = high
    w2[rank : 2 * rank, :] = low
    k3f[...] = jnp.zeros_like(k3f)
    for i in range(4):
        k3f[i * depth : (i + 1) * depth, i * tdim : (i + 1) * tdim] = b3_ref[...]
    high, low = split(k3f[...])
    k3[0] = high
    k3[1] = low

    def contract(k):
        @pl.loop(0, pairs // 2, unroll=True)
        def _(j):
            base = k * step + 2 * j
            parts = []
            for v in range(nv):
                tile = jnp.concatenate(
                    [fbuf[v, base + o] for o in (0, pairs, 1, pairs + 1)], axis=0
                )
                high, low = split(tile)
                one = mul_t(w2[...], high)
                two = mul_t(w2[0:rank, :], low)
                parts.append(one[0:rank] + one[rank:] + two)
            high, low = split(jnp.concatenate(parts, axis=0))
            c = mul(high, k3[0]) + (mul(high, k3[1]) + mul(low, k3[0]))
            for z in range(GZ):
                for v in range(nv):
                    piece = c[v * rank + z * sloc : v * rank + (z + 1) * sloc]
                    core[k, z, v, 2 * j] = piece[:, 0:LANES]
                    core[k, z, v, 2 * j + 1] = piece[:, LANES:]

    def gz_copies(k):
        out = []
        for d in range(1, GZ):
            peer = lax.rem(gz + d, GZ)
            out.append(
                pltpu.make_async_remote_copy(
                    src_ref=core.at[k, peer], dst_ref=rgz.at[k, d - 1],
                    send_sem=zs.at[k, d - 1], recv_sem=zr.at[k, d - 1],
                    device_id=(gx, gy, peer), device_id_type=MESH,
                )
            )
        return out

    def gy_copies(k):
        out = []
        for d in range(1, GY):
            peer = lax.rem(gy + d, GY)
            out.append(
                pltpu.make_async_remote_copy(
                    src_ref=half.at[k, peer], dst_ref=rgy.at[k, d - 1],
                    send_sem=ys.at[k, d - 1], recv_sem=yr.at[k, d - 1],
                    device_id=(gx, peer, gz), device_id_type=MESH,
                )
            )
        return out

    upper = lax.rem(gx + 1, GX)
    across = lax.rem(gx + 2, GX)
    hcols = cols // 2
    sent = pl.multiple_of((across // 2) * hcols, LANES)
    mine = pl.multiple_of((gx // 2) * hcols, LANES)

    def gx_copies(k):
        r = pl.ds(k * step, step)
        return [
            pltpu.make_async_remote_copy(
                src_ref=proj.at[r], dst_ref=q1.at[r],
                send_sem=as_.at[k], recv_sem=ar.at[k],
                device_id=(upper, gy, gz), device_id_type=MESH,
            ),
            pltpu.make_async_remote_copy(
                src_ref=proj.at[r, pl.ds(sent, hcols)], dst_ref=q2.at[r],
                send_sem=bs.at[k], recv_sem=br.at[k],
                device_id=(across, gy, gz), device_id_type=MESH,
            ),
        ]

    zc = [gz_copies(k) for k in range(CHUNKS)]
    yc = [gy_copies(k) for k in range(CHUNKS)]
    xc = [gx_copies(k) for k in range(CHUNKS)]

    def stage_a(k):
        loads[k].wait()
        contract(k)
        if k == 0:
            pl.semaphore_wait(barrier, nr - 1 + GX - 1)
        for c in zc[k]:
            c.start()

    def stage_b(k):
        for c in zc[k]:
            c.wait_recv()

        @pl.loop(0, nv)
        def _(v):
            total = core[k, gz, v]
            for d in range(GZ - 1):
                total = total + rgz[k, d, v]
            half[k, v] = total

        for c in yc[k]:
            c.start()

    def stage_c(k):
        for c in yc[k]:
            c.wait_recv()
        total = half[k, gy]
        for d in range(GY - 1):
            total = total + rgy[k, d]
        xbuf[...] = total.reshape(pairs * sloc, LANES)
        lane = lax.broadcasted_iota(jnp.int32, (pairs, LANES), 1)
        first = lane < tdim
        for p in range(sloc // 2):
            a = xbuf[pl.ds(2 * p, pairs, stride=sloc), :]
            b = xbuf[pl.ds(2 * p + 1, pairs, stride=sloc), :]
            at = pl.ds(p * LANES, LANES)
            proj[pl.ds(k * step, pairs), at] = jnp.where(first, a, pltpu.roll(b, tdim, 1))
            proj[pl.ds(k * step + pairs, pairs), at] = jnp.where(
                first, pltpu.roll(a, tdim, 1), b
            )
        for c in xc[k]:
            c.start()

    for k in range(CHUNKS + LAG):
        if k < CHUNKS:
            stage_a(k)
        if 1 <= k <= CHUNKS:
            stage_b(k - 1)
        if k >= LAG:
            stage_c(k - LAG)

    ph, pw = split(proj[...])
    hh, hw = split(proj[:, pl.ds(mine, hcols)])
    diag = mul_t(ph, ph) + (mul_t(ph, pw) + mul_t(pw, ph))
    for k in range(CHUNKS):
        for c in xc[k]:
            c.wait_recv()
    qh, qw = split(q1[...])
    n1 = mul_t(ph, qh) + (mul_t(ph, qw) + mul_t(pw, qh))
    n1t = mul_t(qh, ph) + (mul_t(qw, ph) + mul_t(qh, pw))
    qh, qw = split(q2[...])
    n2 = mul_t(hh, qh) + (mul_t(hh, qw) + mul_t(hw, qh))
    n2t = mul_t(qh, hh) + (mul_t(qw, hh) + mul_t(qh, hw))
    tbuf[...] = jnp.concatenate([n1t, n2t], axis=1)
    lower = lax.rem(gx + GX - 1, GX)
    swaps = [
        pltpu.make_async_remote_copy(
            src_ref=tbuf, dst_ref=t1, send_sem=ts.at[0], recv_sem=tr.at[0],
            device_id=(lower, gy, gz), device_id_type=MESH,
        ),
        pltpu.make_async_remote_copy(
            src_ref=tbuf, dst_ref=t2, send_sem=ts.at[1], recv_sem=tr.at[1],
            device_id=(across, gy, gz), device_id_type=MESH,
        ),
    ]
    for c in swaps:
        c.start()
    for c in swaps:
        c.wait_recv()
    r1 = t1[:, 0:rows]
    n2 = n2 + t2[:, rows:]
    blocks = []
    for j in range(GX):
        d = lax.rem(j - gx + GX, GX)
        blocks.append(
            jnp.where(d == 0, diag, jnp.where(d == 1, r1, jnp.where(d == 2, n2, n1)))
        )
    whole = jnp.concatenate(blocks, axis=1) * F32(1.0 / (nv * rank * tdim))
    for r in range(nr):
        gp[r] = whole[r * slab : (r + 1) * slab]
    gather = []
    for d in range(1, nr):
        other, where = layer(d)
        gather.append(
            pltpu.make_async_remote_copy(
                src_ref=gp.at[other], dst_ref=rg.at[d - 1],
                send_sem=gs.at[d - 1], recv_sem=gr.at[d - 1],
                device_id=where, device_id_type=MESH,
            )
        )
    for c in gather:
        c.start()
    for c in gather:
        c.wait_recv()
    total = gp[me]
    for d in range(nr - 1):
        total = total + rg[d]
    fin[me] = total
    spread = []
    for d in range(1, nr):
        other, where = layer(d)
        spread.append(
            pltpu.make_async_remote_copy(
                src_ref=fin.at[me], dst_ref=fin.at[me],
                send_sem=hs.at[d - 1], recv_sem=hr.at[d - 1],
                device_id=where, device_id_type=MESH,
            )
        )
    for c in spread:
        c.start()
    for c in spread:
        c.wait_recv()
    for r in range(nr):
        gram[r * slab : (r + 1) * slab, :] = fin[r]
    for group in zc + yc + xc + [swaps, gather, spread]:
        for c in group:
            c.wait_send()


def settle(proj_in, gram_in, proj, gram):
    proj[...] = proj_in[...]
    gram[...] = gram_in[...]


def body(gsize, field, basis_two, basis_three):
    nv, rows, depth, width = field.shape
    rank, tdim = basis_two.shape[1], basis_three.shape[1]
    GX, GY, GZ = gsize
    assert GX == 4 and GY == nv and 4 * depth == 256 and 2 * tdim == LANES
    sloc = rank // GZ
    cols = sloc * tdim
    step = rows // CHUNKS
    pairs = step // 2
    nr = GY * GZ
    slab = rows // nr
    dma = pltpu.SemaphoreType.DMA
    vmem = pl.BlockSpec(memory_space=pltpu.VMEM)
    results = pl.pallas_call(
        functools.partial(kernel, field.shape, gsize),
        out_shape=(
            jax.ShapeDtypeStruct((rows, cols), F32),
            jax.ShapeDtypeStruct((rows, GX * rows), F32),
        ),
        in_specs=[pl.BlockSpec(memory_space=pl.ANY), vmem, vmem],
        out_specs=(vmem, vmem),
        scratch_shapes=[
            pltpu.VMEM(field.shape, F32),
            pltpu.VMEM((2 * rank, width), BF16),
            pltpu.VMEM((2, 4 * depth, 4 * tdim), BF16),
            pltpu.VMEM((4 * depth, 4 * tdim), F32),
            pltpu.VMEM((CHUNKS, GZ, nv, pairs, sloc, LANES), F32),
            pltpu.VMEM((CHUNKS, GZ - 1, nv, pairs, sloc, LANES), F32),
            pltpu.VMEM((CHUNKS, nv, pairs, sloc, LANES), F32),
            pltpu.VMEM((CHUNKS, GY - 1, pairs, sloc, LANES), F32),
            pltpu.VMEM((pairs * sloc, LANES), F32),
            pltpu.VMEM((rows, cols), F32),
            pltpu.VMEM((rows, cols // 2), F32),
            pltpu.VMEM((rows, 2 * rows), F32),
            pltpu.VMEM((rows, 2 * rows), F32),
            pltpu.VMEM((rows, 2 * rows), F32),
            pltpu.VMEM((nr, slab, GX * rows), F32),
            pltpu.VMEM((nr - 1, slab, GX * rows), F32),
            pltpu.VMEM((nr, slab, GX * rows), F32),
            dma((CHUNKS,)),
            dma((CHUNKS, GZ - 1)),
            dma((CHUNKS, GZ - 1)),
            dma((CHUNKS, GY - 1)),
            dma((CHUNKS, GY - 1)),
            dma((CHUNKS,)),
            dma((CHUNKS,)),
            dma((CHUNKS,)),
            dma((CHUNKS,)),
            dma((2,)),
            dma((2,)),
            dma((nr - 1,)),
            dma((nr - 1,)),
            dma((nr - 1,)),
            dma((nr - 1,)),
        ],
        compiler_params=pltpu.CompilerParams(
            collective_id=0, has_side_effects=True, vmem_limit_bytes=56 * 2**20
        ),
    )(field, basis_two.T, basis_three)
    return pl.pallas_call(
        settle,
        out_shape=tuple(jax.ShapeDtypeStruct(r.shape, r.dtype) for r in results),
        in_specs=[vmem, vmem],
        out_specs=(vmem, vmem),
    )(*results)


def solution(mesh):
    placed = (P(None, "gx", "gz", "gy"), P("gy", None), P("gz", None))
    gsize = tuple(mesh.shape[name] for name in ("gx", "gy", "gz"))
    return jax.shard_map(
        functools.partial(body, gsize),
        mesh=mesh,
        in_specs=placed,
        out_specs=(P("gx", ("gy", "gz")), P("gx", None)),
        check_vma=False,
    )
```
